32 devices in a mesh: ctx: 8 (over z, core), ch: 4 (over y, x).
Axes of the slice: x: 2, y: 2, z: 4, core: 2. Of those that a mesh axis runs over, the one named last changes fastest.
Arguments:
- output_gate: bfloat16 [4096, 4096], P('ctx', 'ch'), may hold values from -6 to 6
- input_gate: bfloat16 [4096, 4096], P('ctx', 'ch'), may hold values from -6 to 6
- value_input: bfloat16 [4096, 4096], P('ctx', 'ch'), may hold values from -6 to 6
- short_filter: float32 [128, 4096], P(None, 'ch'), may hold values from -0.5 to 0.5
- long_filter: float32 [4096, 256], P('ctx', 'ch'), may hold values from -0.09375 to 0.09375
- skip_gain: float32 [4096], P('ch'), may hold values from -4 to 4
Outputs:
- mixed: bfloat16 [4096, 4096], P('ctx', 'ch')
The draws below stay inside these ranges and needn't reach their ends.
All inputs are finite; a program needn't handle non-finite values.
Results may differ from the reference program's by a relative error of at most 0.001.
Values may be sent and summed in bfloat16 or wider, within the bound.
No kernel may reach another device: no remote copies, remote signals or barrier semaphores. Data moves between devices by JAX's collectives and lax.ppermute only.
A program may use at most 64 MiB of HBM per device.

```python
import math
import jax
import jax.numpy as jnp
from jax import lax

D = 4096
GROUP = 16
SHORT = 128
TOKENS = 4096
FILTERS = 256


def block_scale(key, shape, pieces, smallest, top_value):
    def one(axis_at, shards_of):
        heights = jax.random.uniform(jax.random.fold_in(jax.random.fold_in(key, 6), axis_at), (shards_of,), jnp.float32, smallest / len(pieces), top_value / len(pieces))
        return jnp.repeat(jnp.exp(heights), shape[axis_at] // shards_of).reshape((-1,) + (1,) * (len(shape) - axis_at - 1))

    gain = one(*pieces[0])
    for cut in pieces[1:]:
        gain = gain * one(*cut)
    return gain


def noise(rng, shape, deviation, reach, pieces=(), kind=jnp.bfloat16):
    values = deviation * jax.random.normal(rng, shape, jnp.float32)
    if pieces:
        values = values * block_scale(rng, shape, pieces, -0.22, 0.18)
    return jnp.clip(values, -reach, reach).astype(kind)


def setup_inputs(seed: int = 0) -> dict:
    keys = jax.random.split(jax.random.key(seed), 7)
    output_gate = noise(keys[0], (TOKENS, D), 1.0, 6.0, ((0, 8), (1, 4)))
    input_gate = noise(keys[1], (TOKENS, D), 1.0, 6.0, ((0, 8), (1, 4)))
    value_input = noise(keys[2], (TOKENS, D), 1.0, 6.0, ((0, 8), (1, 4)))
    short_filter = noise(keys[3], (SHORT, D), SHORT ** -0.5, 0.5, ((1, 4),), jnp.float32)
    long_filter = noise(keys[4], (TOKENS, FILTERS), TOKENS ** -0.5, 0.09375, ((0, 8), (1, 4)), jnp.float32)
    skip_gain = noise(keys[5], (D,), 1.0, 4.0, ((0, 4),), jnp.float32)
    return {"output_gate": output_gate, "input_gate": input_gate, "value_input": value_input, "short_filter": short_filter, "long_filter": long_filter, "skip_gain": skip_gain}


def causal_short(signal, filter_taps):
    tap_count = filter_taps.shape[0]
    length = signal.shape[0]
    padded = jnp.pad(signal, ((tap_count - 1, 0), (0, 0)))

    def add_tap(tap, total):
        start = (tap_count - 1 - tap).astype(jnp.int32)
        rows = lax.dynamic_slice_in_dim(padded, start, length, 0)
        taps = lax.dynamic_slice_in_dim(filter_taps, tap.astype(jnp.int32), 1, 0)
        return total + rows * taps

    return lax.fori_loop(0, tap_count, add_tap, jnp.zeros_like(signal))


def long_conv(gated, long_filter):
    length = gated.shape[0]
    fft_length = 2 * length
    block_count = math.gcd(long_filter.shape[1], 16)
    filter_spec = jnp.fft.rfft(long_filter, n=fft_length, axis=0)
    signal_blocks = jnp.moveaxis(gated.reshape(length, block_count, -1), 1, 0)
    filter_blocks = jnp.moveaxis(filter_spec.reshape(filter_spec.shape[0], block_count, -1), 1, 0)

    def one_block(pair):
        signal, spectrum = pair
        signal_spec = jnp.fft.rfft(signal, n=fft_length, axis=0)
        widened = jnp.repeat(spectrum, GROUP, axis=1)
        return jnp.fft.irfft(signal_spec * widened, n=fft_length, axis=0)[:length]

    result = lax.map(one_block, (signal_blocks, filter_blocks))
    return jnp.moveaxis(result, 0, 1).reshape(length, -1)


def reference(output_gate, input_gate, value_input, short_filter, long_filter, skip_gain):
    short_out = causal_short(value_input.astype(jnp.float32), short_filter)
    gated = input_gate.astype(jnp.float32) * short_out
    long_out = long_conv(gated, long_filter)
    mixed = output_gate.astype(jnp.float32) * (long_out + skip_gain[None, :] * gated)
    return mixed.astype(jnp.bfloat16)
```

```python
import functools
import math

import jax
import jax.numpy as jnp
import numpy as np
from jax import lax
from jax.experimental import pallas as pl
from jax.experimental.pallas import tpu as pltpu
from jax.sharding import PartitionSpec as P

HIGHEST = lax.Precision.HIGHEST
LANES = 128
TILE = 16
SPAN = 250.0
BIAS = 125.0
TINY = 1e-30
MIB = 1 << 20


def passed_along(block, axis, distance):
    devices = range(lax.axis_size(axis))
    route = [(i - distance, i) for i in devices if i - distance in devices]
    return lax.ppermute(block, axis, route)


def depthwise(extended, filter_taps):
    kernel = filter_taps[::-1][:, None, :]
    result = lax.conv_general_dilated(
        extended[None],
        kernel,
        (1,),
        "VALID",
        dimension_numbers=("NWC", "WIO", "NWC"),
        feature_group_count=extended.shape[1],
        precision=HIGHEST,
    )
    return result[0]


def rotate(real_part, imag_part, cosine, sine):
    return (real_part * cosine - imag_part * sine, real_part * sine + imag_part * cosine)


def table_apply(pattern, cosine, sine, real_part, imag_part):
    out_real = jnp.einsum(pattern, cosine, real_part, precision=HIGHEST) - jnp.einsum(
        pattern, sine, imag_part, precision=HIGHEST
    )
    out_imag = jnp.einsum(pattern, cosine, imag_part, precision=HIGHEST) + jnp.einsum(
        pattern, sine, real_part, precision=HIGHEST
    )
    return (out_real, out_imag)


def dft_table(length, sign):
    index_vals = jnp.arange(length, dtype=jnp.int32)
    exponent = index_vals[:, None] * index_vals[None, :] % length
    angle = sign * 2.0 * math.pi * exponent.astype(jnp.float32) / length
    return (jnp.cos(angle), jnp.sin(angle))


def channel_local(signal, filt):
    length, cols = signal.shape
    fft_length = 2 * length
    size_a = math.gcd(length, 1 << fft_length.bit_length() // 2)
    size_b = fft_length // size_a
    half_b = size_b // 2
    pair_cols = cols // 2
    paired = signal.reshape(half_b, size_a, pair_cols, 2)
    sig_real = paired[..., 0]
    sig_imag = paired[..., 1]
    filt_real = filt.reshape(half_b, size_a, pair_cols, 2)[..., 0]
    b_cos, b_sin = dft_table(size_b, -1.0)
    in_cos = b_cos[:, :half_b]
    in_sin = b_sin[:, :half_b]
    data_real, data_imag = table_apply("kb,bap->kap", in_cos, in_sin, sig_real, sig_imag)
    spec_real = jnp.einsum("kb,bap->kap", in_cos, filt_real, precision=HIGHEST)
    spec_imag = jnp.einsum("kb,bap->kap", in_sin, filt_real, precision=HIGHEST)
    fine_index = jnp.arange(size_b, dtype=jnp.int32)
    coarse_index = jnp.arange(size_a, dtype=jnp.int32)
    exponent = fine_index[:, None] * coarse_index[None, :] % fft_length
    tw_angle = -2.0 * math.pi * exponent.astype(jnp.float32) / fft_length
    tw_cos = jnp.cos(tw_angle)[:, :, None]
    tw_sin = jnp.sin(tw_angle)[:, :, None]
    data_real, data_imag = rotate(data_real, data_imag, tw_cos, tw_sin)
    spec_real, spec_imag = rotate(spec_real, spec_imag, tw_cos, tw_sin)
    a_cos, a_sin = dft_table(size_a, -1.0)
    data_real, data_imag = table_apply("ka,bap->bkp", a_cos, a_sin, data_real, data_imag)
    spec_real, spec_imag = table_apply("ka,bap->bkp", a_cos, a_sin, spec_real, spec_imag)
    prod_real = data_real * spec_real - data_imag * spec_imag
    prod_imag = data_real * spec_imag + data_imag * spec_real
    back_real, back_imag = table_apply("ak,bkp->bap", a_cos, -a_sin, prod_real, prod_imag)
    back_real, back_imag = rotate(back_real, back_imag, tw_cos, -tw_sin)
    final_real, final_imag = table_apply(
        "bk,kap->bap", b_cos[:half_b], -b_sin[:half_b], back_real, back_imag
    )
    joined = jnp.stack([final_real, final_imag], axis=-1).reshape(length, cols)
    return joined / fft_length


def plain(output_gate, input_gate, value_input, short_filter, long_filter, skip_gain):
    row_count, chan_count = value_input.shape
    group_total = long_filter.shape[1]
    tap_count = short_filter.shape[0]
    earlier = passed_along(value_input[row_count - tap_count + 1 :], "ctx", 1)
    extended = jnp.concatenate([earlier, value_input], axis=0).astype(jnp.float32)
    gated = input_gate.astype(jnp.float32) * depthwise(extended, short_filter)
    widened = jnp.repeat(long_filter, chan_count // group_total, axis=1)
    moved = (
        lax.all_to_all(gated, "ctx", split_axis=1, concat_axis=0, tiled=True),
        lax.all_to_all(widened, "ctx", split_axis=1, concat_axis=0, tiled=True),
    )
    convolved = channel_local(moved[0], moved[1])
    long_out = lax.all_to_all(convolved, "ctx", split_axis=0, concat_axis=1, tiled=True)
    mixed = output_gate.astype(jnp.float32) * (long_out + skip_gain[None, :] * gated)
    return mixed.astype(jnp.bfloat16)


def split(values):
    high = values.astype(jnp.bfloat16)
    return high, (values - high.astype(jnp.float32)).astype(jnp.bfloat16)


def split_table(table):
    high = table.astype(np.float32).astype(jnp.bfloat16)
    low = (table - high.astype(np.float64)).astype(np.float32).astype(jnp.bfloat16)
    return np.stack([high, low])


@functools.lru_cache
def tables(half):
    bins = np.arange(half)[:, None] + 0.5
    angle = 2.0 * np.pi * bins * np.arange(2 * half)[None, :] / (2 * half)
    forward = np.concatenate([np.cos(angle), -np.sin(angle)], 0)
    return forward, forward.T / half


def widening(groups, lanes):
    one = np.kron(np.eye(groups), np.ones((1, lanes // groups)))
    return np.kron(np.eye(2), one).astype(jnp.bfloat16)


def dot(a, b):
    return jnp.dot(a, b, preferred_element_type=jnp.float32)


def dot3(table, values):
    high, low = split(values)
    cols = values.shape[1]
    both = dot(table[0], jnp.concatenate([high, low], 1))
    return both[:, :cols] + both[:, cols:] + dot(table[1], high)


def scale_of(top):
    return jnp.maximum(top * 1.01, TINY).astype(jnp.bfloat16).astype(jnp.float32)


def to_code(values, scale):
    power = jnp.exp2(jnp.abs(values) * (SPAN / scale) - BIAS)
    return jnp.where(values < 0.0, -power, power).astype(jnp.bfloat16)


def from_code(code, scale):
    power = code.astype(jnp.float32)
    size = (jnp.log(jnp.abs(power)) * (1.0 / math.log(2.0)) + BIAS) * (scale * (1.0 / SPAN))
    return jnp.where(power < 0.0, -size, size)


def short_rows(ext, taps_spec, fwd, inv):
    count = taps_spec.shape[0] // 2
    rows, cols = ext.shape
    starts = range(0, rows - count, count)
    wide = jnp.concatenate([ext[s : s + 2 * count] for s in starts], 1)
    spec = dot(fwd[0], wide) + dot(fwd[1], wide)
    t_re = jnp.concatenate([taps_spec[:count]] * len(starts), 1)
    t_im = jnp.concatenate([taps_spec[count:]] * len(starts), 1)
    s_re, s_im = spec[:count], spec[count:]
    prod = jnp.concatenate([s_re * t_re - s_im * t_im, s_re * t_im + s_im * t_re], 0)
    back = dot3(inv, prod)
    return jnp.concatenate([back[:, w * cols : (w + 1) * cols] for w in range(len(starts))], 0)


IN_VMEM = pl.BlockSpec(memory_space=pltpu.VMEM)
IN_SMEM = pl.BlockSpec(memory_space=pltpu.SMEM)
IN_ANY = pl.BlockSpec(memory_space=pl.ANY)


def kernel_params(mib):
    return pltpu.CompilerParams(vmem_limit_bytes=mib * MIB)


def cost(scale):
    return pl.CostEstimate(flops=scale * 1_000_000, bytes_accessed=scale * 1000, transcendentals=0)


def lanes_of(slab):
    return pl.ds(pl.multiple_of(slab * LANES, LANES), LANES)


def main_body(value, gate, taps, fwd, inv, gated, spec_out):
    count = taps.shape[0]
    wide = 2 * LANES
    for c in range(0, value.shape[1], wide):
        cols = slice(c, c + wide)
        taps_spec = dot3(fwd[:, :, :count], taps[:, cols])
        spec_out[:, cols] = taps_spec
        short = short_rows(value[:, cols], taps_spec, fwd, inv)
        gated[:, cols] = gate[count:, cols].astype(jnp.float32) * short


def main_call(value, gate, taps, fwd, inv):
    rows, chans = value.shape
    count = taps.shape[0]
    return pl.pallas_call(
        main_body,
        in_specs=[IN_VMEM] * 5,
        out_specs=[IN_VMEM] * 2,
        out_shape=[
            jax.ShapeDtypeStruct((rows - count, chans), jnp.float32),
            jax.ShapeDtypeStruct((2 * count, chans), jnp.float32),
        ],
        compiler_params=kernel_params(12),
        cost_estimate=cost(4),
        name="short_main",
    )(value, gate, taps, fwd, inv)


def head_body(part, count, me, halo, value, gate, gated, taps_spec, long_taps, fwd, inv, *outs):
    taps = halo.shape[0]
    rows = taps + gated.shape[0]
    groups = 8
    tops, codes = outs[: len(part)], outs[len(part) :]
    for d, top, code in zip(part, tops, codes):
        slab = lax.rem(me[0] + d, count)
        cols = lanes_of(slab)
        ext = jnp.concatenate([halo[:, cols], value[:taps, cols]], 0)
        short = short_rows(ext, taps_spec[:, cols], fwd, inv)
        first = gate[:taps, cols].astype(jnp.float32) * short
        top[...] = first
        later = gated[:, cols]
        peak = jnp.maximum(
            jnp.max(jnp.abs(first), axis=0, keepdims=True),
            jnp.max(jnp.abs(later), axis=0, keepdims=True),
        )
        scale = scale_of(peak)
        held = long_taps[slab]
        size = jnp.abs(held)
        most = size[:groups]
        for c in range(groups, held.shape[0], groups):
            most = jnp.maximum(most, size[c : c + groups])
        filter_scale = scale_of(jnp.max(most, axis=1, keepdims=True))
        filter_scale = jnp.broadcast_to(filter_scale, (groups, LANES))
        many = held.shape[0] // groups
        code[:taps] = to_code(first, scale)
        code[taps:rows] = to_code(later, scale)
        both = jnp.concatenate([jnp.broadcast_to(scale, (8, LANES)), filter_scale], 0)
        code[rows : rows + TILE] = both.astype(jnp.bfloat16)
        code[rows + TILE :] = to_code(held, jnp.concatenate([filter_scale] * many, 0))


def head_call(part, count, me, halo, value, gate, gated, taps_spec, long_taps, fwd, inv):
    taps = halo.shape[0]
    rows = taps + gated.shape[0]
    held = long_taps.shape[1]
    code = jax.ShapeDtypeStruct((rows + TILE + held, LANES), jnp.bfloat16)
    top = jax.ShapeDtypeStruct((taps, LANES), jnp.float32)
    return pl.pallas_call(
        functools.partial(head_body, part, count),
        in_specs=[IN_SMEM] + [IN_VMEM] * 8,
        out_specs=[IN_VMEM] * (2 * len(part)),
        out_shape=[top] * len(part) + [code] * len(part),
        compiler_params=kernel_params(12),
        cost_estimate=cost(len(part)),
        name="short_head",
    )(me, halo, value, gate, gated, taps_spec, long_taps, fwd, inv)


def forward_body(code, fwd, widen, spec_out, filter_out):
    rows = fwd.shape[2]
    groups = 8
    x_high, x_low = split(from_code(code[:rows], code[rows : rows + 1].astype(jnp.float32)))
    scale = code[rows : rows + TILE].astype(jnp.float32)[groups:]
    held = code[rows + TILE :]
    many = held.shape[0] // groups
    h_high, h_low = split(from_code(held, jnp.concatenate([scale] * many, 0)))
    h_high, h_low = h_high.astype(jnp.float32), h_low.astype(jnp.float32)
    parts = []
    for c in range(0, held.shape[0], groups):
        pair = jnp.concatenate([h_high[c : c + groups], h_low[c : c + groups]], 0)
        parts.append(dot(pair.T.astype(jnp.bfloat16), widen[...]).astype(jnp.bfloat16))
    taps = jnp.concatenate(parts, 0)
    x_wide = dot(fwd[0], jnp.concatenate([x_high, x_low], 1))
    h_wide = dot(fwd[0], taps)
    low = dot(fwd[1], jnp.concatenate([x_high, taps[:, :LANES]], 1))
    spec_out[...] = x_wide[:, :LANES] + x_wide[:, LANES:] + low[:, :LANES]
    filter_out[...] = h_wide[:, :LANES] + h_wide[:, LANES:] + low[:, LANES:]


def forward_call(code, fwd, widen):
    bins = fwd.shape[1]
    spec = jax.ShapeDtypeStruct((bins, LANES), jnp.float32)
    return pl.pallas_call(
        forward_body,
        in_specs=[IN_VMEM] * 3,
        out_specs=[IN_VMEM] * 2,
        out_shape=[spec, spec],
        compiler_params=kernel_params(12),
        cost_estimate=cost(1),
        name="forward",
    )(code, fwd, widen)


def by_lag_body(me_ref, *refs):
    spectra, out = refs[:-1], refs[-1]
    count = len(spectra)
    half = out.shape[1] // 2
    me = me_ref[0]
    odd = lax.broadcasted_iota(jnp.int32, (8, LANES), 0) % 2 == 1
    sign = jnp.where(odd, 1.0, -1.0)
    lags = [lax.rem(me - d + count, count) for d in range(count)]
    signs = [sign * (lag > 0).astype(jnp.float32) for lag in lags]

    def chunk(c, _):
        re = pl.ds(pl.multiple_of(c * 8, 8), 8)
        im = pl.ds(pl.multiple_of(half + c * 8, 8), 8)
        for d in range(count):
            before = spectra[(d + 1) % count]
            out[lags[d], re] = spectra[d][re] + signs[d] * before[im]
            out[lags[d], im] = spectra[d][im] - signs[d] * before[re]
        out[count, re] = jnp.zeros((8, LANES), jnp.float32)
        out[count, im] = jnp.zeros((8, LANES), jnp.float32)
        return 0

    lax.fori_loop(0, half // 8, chunk, 0, unroll=2)


def by_lag_call(me, spectra):
    count = len(spectra)
    bins = spectra[0].shape[0]
    return pl.pallas_call(
        by_lag_body,
        in_specs=[IN_SMEM] + [IN_VMEM] * count,
        out_specs=IN_VMEM,
        out_shape=jax.ShapeDtypeStruct((count + 1, bins, LANES), jnp.float32),
        compiler_params=kernel_params(12),
        cost_estimate=cost(1),
        name="by_lag",
    )(me, *spectra)


def back_body(part, count, me_ref, filt, inv, *refs):
    specs, codes, total = refs[:count], refs[-1 - len(part) : -1], refs[-1]
    half = filt.shape[1] // 2
    rows = inv.shape[1]
    me = me_ref[0]

    for e, code in zip(part, codes):
        target = lax.rem(me + e, count)
        lags = []
        for d in range(count):
            lag = target - lax.rem(me - d + count, count)
            lags.append(jnp.where(lag >= 0, lag, count))

        def chunk(c, _):
            re = pl.ds(pl.multiple_of(c * 8, 8), 8)
            im = pl.ds(pl.multiple_of(half + c * 8, 8), 8)
            acc_re = jnp.zeros((8, LANES), jnp.float32)
            acc_im = acc_re
            for d in range(count):
                x_re, x_im = specs[d][re], specs[d][im]
                g_re, g_im = filt[lags[d], re], filt[lags[d], im]
                acc_re += x_re * g_re - x_im * g_im
                acc_im += x_re * g_im + x_im * g_re
            total[re] = acc_re
            total[im] = acc_im
            return 0

        lax.fori_loop(0, half // 8, chunk, 0, unroll=2)
        values = dot3(inv, total[...])
        scale = scale_of(jnp.max(jnp.abs(values), axis=0, keepdims=True))
        code[:rows] = to_code(values, scale)
        code[rows:] = jnp.broadcast_to(scale, (TILE, LANES)).astype(jnp.bfloat16)


def back_call(part, me, filt, inv, specs, after):
    count = len(specs)
    bins = specs[0].shape[0]
    code = jax.ShapeDtypeStruct((bins // 2 + TILE, LANES), jnp.bfloat16)
    return pl.pallas_call(
        functools.partial(back_body, part, count),
        in_specs=[IN_SMEM] + [IN_VMEM] * (2 + count) + [IN_ANY] * len(after),
        out_specs=[IN_VMEM] * len(part),
        out_shape=[code] * len(part),
        scratch_shapes=[pltpu.VMEM((bins, LANES), jnp.float32)],
        compiler_params=kernel_params(12),
        cost_estimate=cost(len(part)),
        name="back",
    )(me, filt, inv, *specs, *after)


def final_body(part, count, me, *refs):
    many = len(part)
    codes, tops, (gated, gate, skip) = refs[:many], refs[many : 2 * many], refs[2 * many : 2 * many + 3]
    out, held, sems = refs[-3:]
    taps = tops[0].shape[0]
    rows = gate.shape[0]
    copies = []
    for at, d in enumerate(part):
        cols = lanes_of(lax.rem(me[0] + d, count))
        code, top = codes[at], tops[at]
        scale = code[rows : rows + 1].astype(jnp.float32)
        for r, part_gated in ((slice(0, taps), top[...]), (slice(taps, rows), gated[:, cols])):
            total = from_code(code[r], scale) + skip[:, cols] * part_gated
            held[at, r] = (gate[r, cols].astype(jnp.float32) * total).astype(jnp.bfloat16)
        copies.append(pltpu.make_async_copy(held.at[at], out.at[:, cols], sems.at[at]))
        copies[-1].start()
    for copy in copies:
        copy.wait()


def final_call(part, count, me, codes, tops, gated, gate, skip, so_far):
    rows = gate.shape[0]
    many = len(part)
    args = [me, *codes, *tops, gated, gate, skip]
    specs = [IN_SMEM] + [IN_VMEM] * (2 * many + 3)
    alias = {}
    if so_far is not None:
        alias = {len(args): 0}
        args.append(so_far)
        specs.append(IN_ANY)
    return pl.pallas_call(
        functools.partial(final_body, part, count),
        in_specs=specs,
        out_specs=IN_ANY,
        out_shape=jax.ShapeDtypeStruct(gate.shape, jnp.bfloat16),
        scratch_shapes=[
            pltpu.VMEM((many, rows, LANES), jnp.bfloat16),
            pltpu.SemaphoreType.DMA((many,)),
        ],
        input_output_aliases=alias,
        compiler_params=kernel_params(12),
        cost_estimate=cost(many),
        name="final",
    )(*args)


def rotation_order(count):
    return sorted(range(1, count), key=lambda d: (-min(d, count - d), d))


def in_slabs(output_gate, input_gate, value_input, short_filter, long_filter, skip_gain):
    count = lax.axis_size("ctx")
    me = lax.axis_index("ctx").reshape(1)
    rows = value_input.shape[0]
    taps = short_filter.shape[0]
    groups = long_filter.shape[1] // count
    order = rotation_order(count) + [0]

    def rotated(block, distance):
        return lax.ppermute(block, "ctx", [(i, (i + distance) % count) for i in range(count)])

    def table(values):
        return jnp.asarray(split_table(values))

    halo = passed_along(value_input[rows - taps :], "ctx", 1)
    long_taps = long_filter.T.reshape(count, groups, rows // LANES, LANES)
    long_taps = jnp.swapaxes(long_taps, 1, 2).reshape(count, -1, LANES)

    forward, inverse = tables(taps)
    short_fwd, short_inv = table(forward), table(inverse[taps:])
    forward, inverse = tables(rows)
    fwd, inv = table(forward[:, :rows]), table(inverse[:rows])
    widen = jnp.asarray(widening(groups, LANES))

    gated, taps_spec = main_call(value_input, input_gate, short_filter, short_fwd, short_inv)
    came, tops = {}, {}
    for part in (order[:1], order[1:3], order[3:]):
        outs = head_call(
            part, count, me, halo, value_input, input_gate, gated, taps_spec, long_taps,
            short_fwd, short_inv,
        )
        for d, top, code in zip(part, outs, outs[len(part) :]):
            tops[d] = top
            came[d] = rotated(code, d) if d else code

    specs, spectra = [None] * count, [None] * count
    for d in order[-1:] + order[:-1]:
        specs[d], spectra[d] = forward_call(came[d], fwd, widen)
    filt = by_lag_call(me, spectra)

    answers, after = {}, []
    for part in (order[:1], order[1:3], order[3:]):
        codes = back_call(part, me, filt, inv, specs, after)
        for e, code in zip(part, codes):
            answers[e] = rotated(code, e) if e else code
        after = codes[:1]

    mixed = None
    for part in (order[-1:] + order[:3], order[3:6], order[6:-1]):
        owners = [(count - e) % count for e in part]
        mixed = final_call(
            owners, count, me, [answers[e] for e in part], [tops[d] for d in owners], gated,
            output_gate, skip_gain[None], mixed,
        )
    return mixed


def local(output_gate, input_gate, value_input, short_filter, long_filter, skip_gain):
    count = lax.axis_size("ctx")
    rows, chans = value_input.shape
    taps = short_filter.shape[0]
    groups = long_filter.shape[1]
    fits = chans == LANES * count and groups == 8 * count and taps == LANES
    fits = fits and rows % taps == 0 and rows > taps
    run = in_slabs if fits else plain
    return run(output_gate, input_gate, value_input, short_filter, long_filter, skip_gain)


def solution(mesh):
    placed = (
        P("ctx", "ch"),
        P("ctx", "ch"),
        P("ctx", "ch"),
        P(None, "ch"),
        P("ctx", "ch"),
        P("ch"),
    )
    return jax.shard_map(
        local, mesh=mesh, in_specs=placed, out_specs=P("ctx", "ch"), check_vma=False
    )
```

```python
import functools
import math

import jax
import jax.numpy as jnp
import numpy as np
from jax import lax
from jax.experimental import pallas as pl
from jax.experimental.pallas import tpu as pltpu
from jax.sharding import PartitionSpec as P

HIGHEST = lax.Precision.HIGHEST
LANES = 128
TILE = 16
SPAN = 250.0
BIAS = 125.0
TINY = 1e-30
MIB = 1 << 20


def passed_along(block, axis, distance):
    devices = range(lax.axis_size(axis))
    route = [(i - distance, i) for i in devices if i - distance in devices]
    return lax.ppermute(block, axis, route)


def depthwise(extended, filter_taps):
    kernel = filter_taps[::-1][:, None, :]
    result = lax.conv_general_dilated(
        extended[None],
        kernel,
        (1,),
        "VALID",
        dimension_numbers=("NWC", "WIO", "NWC"),
        feature_group_count=extended.shape[1],
        precision=HIGHEST,
    )
    return result[0]


def rotate(real_part, imag_part, cosine, sine):
    return (real_part * cosine - imag_part * sine, real_part * sine + imag_part * cosine)


def table_apply(pattern, cosine, sine, real_part, imag_part):
    out_real = jnp.einsum(pattern, cosine, real_part, precision=HIGHEST) - jnp.einsum(
        pattern, sine, imag_part, precision=HIGHEST
    )
    out_imag = jnp.einsum(pattern, cosine, imag_part, precision=HIGHEST) + jnp.einsum(
        pattern, sine, real_part, precision=HIGHEST
    )
    return (out_real, out_imag)


def dft_table(length, sign):
    index_vals = jnp.arange(length, dtype=jnp.int32)
    exponent = index_vals[:, None] * index_vals[None, :] % length
    angle = sign * 2.0 * math.pi * exponent.astype(jnp.float32) / length
    return (jnp.cos(angle), jnp.sin(angle))


def channel_local(signal, filt):
    length, cols = signal.shape
    fft_length = 2 * length
    size_a = math.gcd(length, 1 << fft_length.bit_length() // 2)
    size_b = fft_length // size_a
    half_b = size_b // 2
    pair_cols = cols // 2
    paired = signal.reshape(half_b, size_a, pair_cols, 2)
    sig_real = paired[..., 0]
    sig_imag = paired[..., 1]
    filt_real = filt.reshape(half_b, size_a, pair_cols, 2)[..., 0]
    b_cos, b_sin = dft_table(size_b, -1.0)
    in_cos = b_cos[:, :half_b]
    in_sin = b_sin[:, :half_b]
    data_real, data_imag = table_apply("kb,bap->kap", in_cos, in_sin, sig_real, sig_imag)
    spec_real = jnp.einsum("kb,bap->kap", in_cos, filt_real, precision=HIGHEST)
    spec_imag = jnp.einsum("kb,bap->kap", in_sin, filt_real, precision=HIGHEST)
    fine_index = jnp.arange(size_b, dtype=jnp.int32)
    coarse_index = jnp.arange(size_a, dtype=jnp.int32)
    exponent = fine_index[:, None] * coarse_index[None, :] % fft_length
    tw_angle = -2.0 * math.pi * exponent.astype(jnp.float32) / fft_length
    tw_cos = jnp.cos(tw_angle)[:, :, None]
    tw_sin = jnp.sin(tw_angle)[:, :, None]
    data_real, data_imag = rotate(data_real, data_imag, tw_cos, tw_sin)
    spec_real, spec_imag = rotate(spec_real, spec_imag, tw_cos, tw_sin)
    a_cos, a_sin = dft_table(size_a, -1.0)
    data_real, data_imag = table_apply("ka,bap->bkp", a_cos, a_sin, data_real, data_imag)
    spec_real, spec_imag = table_apply("ka,bap->bkp", a_cos, a_sin, spec_real, spec_imag)
    prod_real = data_real * spec_real - data_imag * spec_imag
    prod_imag = data_real * spec_imag + data_imag * spec_real
    back_real, back_imag = table_apply("ak,bkp->bap", a_cos, -a_sin, prod_real, prod_imag)
    back_real, back_imag = rotate(back_real, back_imag, tw_cos, -tw_sin)
    final_real, final_imag = table_apply(
        "bk,kap->bap", b_cos[:half_b], -b_sin[:half_b], back_real, back_imag
    )
    joined = jnp.stack([final_real, final_imag], axis=-1).reshape(length, cols)
    return joined / fft_length


def plain(output_gate, input_gate, value_input, short_filter, long_filter, skip_gain):
    row_count, chan_count = value_input.shape
    group_total = long_filter.shape[1]
    tap_count = short_filter.shape[0]
    earlier = passed_along(value_input[row_count - tap_count + 1 :], "ctx", 1)
    extended = jnp.concatenate([earlier, value_input], axis=0).astype(jnp.float32)
    gated = input_gate.astype(jnp.float32) * depthwise(extended, short_filter)
    widened = jnp.repeat(long_filter, chan_count // group_total, axis=1)
    moved = (
        lax.all_to_all(gated, "ctx", split_axis=1, concat_axis=0, tiled=True),
        lax.all_to_all(widened, "ctx", split_axis=1, concat_axis=0, tiled=True),
    )
    convolved = channel_local(moved[0], moved[1])
    long_out = lax.all_to_all(convolved, "ctx", split_axis=0, concat_axis=1, tiled=True)
    mixed = output_gate.astype(jnp.float32) * (long_out + skip_gain[None, :] * gated)
    return mixed.astype(jnp.bfloat16)


def split(values):
    high = values.astype(jnp.bfloat16)
    return high, (values - high.astype(jnp.float32)).astype(jnp.bfloat16)


def split_table(table):
    high = table.astype(np.float32).astype(jnp.bfloat16)
    low = (table - high.astype(np.float64)).astype(np.float32).astype(jnp.bfloat16)
    return np.stack([high, low])


@functools.lru_cache
def tables(half):
    bins = np.arange(half)[:, None] + 0.5
    angle = 2.0 * np.pi * bins * np.arange(2 * half)[None, :] / (2 * half)
    forward = np.concatenate([np.cos(angle), -np.sin(angle)], 0)
    return forward, forward.T / half


def turning(rows, lanes):
    angle = 2.0 * np.pi * (np.arange(rows // 2) + 0.5) / (2 * rows)
    both = np.concatenate([np.cos(angle), -np.sin(angle)]).astype(np.float32)
    return np.repeat(both[:, None], lanes, 1)


def widening(groups, lanes):
    one = np.kron(np.eye(groups), np.ones((1, lanes // groups)))
    return np.kron(np.eye(2), one).astype(jnp.bfloat16)


def dot(a, b):
    return jnp.dot(a, b, preferred_element_type=jnp.float32)


def dot3(table, values):
    high, low = split(values)
    cols = values.shape[1]
    both = dot(table[0], jnp.concatenate([high, low], 1))
    return both[:, :cols] + both[:, cols:] + dot(table[1], high)


def scale_of(top):
    return jnp.maximum(top * 1.01, TINY).astype(jnp.bfloat16).astype(jnp.float32)


def to_code(values, scale):
    power = jnp.exp2(jnp.abs(values) * (SPAN / scale) - BIAS)
    return jnp.where(values < 0.0, -power, power).astype(jnp.bfloat16)


def from_code(code, scale):
    power = code.astype(jnp.float32)
    size = (jnp.log(jnp.abs(power)) * (1.0 / math.log(2.0)) + BIAS) * (scale * (1.0 / SPAN))
    return jnp.where(power < 0.0, -size, size)


def short_rows(ext, taps_spec, fwd, inv):
    count = taps_spec.shape[0] // 2
    rows, cols = ext.shape
    starts = range(0, rows - count, count)
    wide = jnp.concatenate([ext[s : s + 2 * count] for s in starts], 1)
    spec = dot(fwd[0], wide) + dot(fwd[1], wide)
    t_re = jnp.concatenate([taps_spec[:count]] * len(starts), 1)
    t_im = jnp.concatenate([taps_spec[count:]] * len(starts), 1)
    s_re, s_im = spec[:count], spec[count:]
    prod = jnp.concatenate([s_re * t_re - s_im * t_im, s_re * t_im + s_im * t_re], 0)
    back = dot3(inv, prod)
    return jnp.concatenate([back[:, w * cols : (w + 1) * cols] for w in range(len(starts))], 0)


IN_VMEM = pl.BlockSpec(memory_space=pltpu.VMEM)
IN_SMEM = pl.BlockSpec(memory_space=pltpu.SMEM)
IN_ANY = pl.BlockSpec(memory_space=pl.ANY)
IN_HBM = pl.BlockSpec(memory_space=pltpu.HBM)


def kernel_params(mib):
    return pltpu.CompilerParams(vmem_limit_bytes=mib * MIB)


def cost(scale):
    return pl.CostEstimate(flops=scale * 1_000_000, bytes_accessed=scale * 1000, transcendentals=0)


def lanes_of(slab):
    return pl.ds(pl.multiple_of(slab * LANES, LANES), LANES)


def tail_body(value, out, sem):
    count = out.shape[0]
    copy = pltpu.make_async_copy(value.at[value.shape[0] - count :], out, sem)
    copy.start()
    copy.wait()


def tail_call(value, count):
    return pl.pallas_call(
        tail_body,
        in_specs=[IN_HBM],
        out_specs=IN_VMEM,
        out_shape=jax.ShapeDtypeStruct((count, value.shape[1]), value.dtype),
        scratch_shapes=[pltpu.SemaphoreType.DMA],
        compiler_params=kernel_params(4),
        cost_estimate=pl.CostEstimate(flops=10_000_000_000, bytes_accessed=1000, transcendentals=0),
        name="tail",
    )(value)


def main_body(value, gate, taps, fwd, inv, gated, spec_out, *scratch):
    tops, held, fwd_held, inv_held = scratch[:2], scratch[2:5], scratch[5], scratch[6]
    sems = scratch[7]
    count = taps.shape[0]
    wide = 2 * LANES
    chunks = [slice(c, c + wide) for c in range(0, value.shape[1], wide)]
    tables_in = [
        pltpu.make_async_copy(fwd, fwd_held, sems.at[0, 0]),
        pltpu.make_async_copy(inv, inv_held, sems.at[0, 1]),
    ]
    pieces = [
        [
            pltpu.make_async_copy(src.at[:, cols], dst.at[:, cols], sems.at[1 + at, k])
            for k, (src, dst) in enumerate(zip((taps, value, gate), held))
        ]
        for at, cols in enumerate(chunks)
    ]
    for copy in sum(pieces[:1], tables_in) + sum(pieces[1:], []):
        copy.start()
    for copy in tables_in:
        copy.wait()
    for at, cols in enumerate(chunks):
        for copy in pieces[at]:
            copy.wait()
        taps_spec = dot3(fwd_held[:, :, :count], held[0][:, cols])
        spec_out[:, cols] = taps_spec
        short = short_rows(held[1][:, cols], taps_spec, fwd_held, inv_held)
        gated[:, cols] = held[2][count:, cols].astype(jnp.float32) * short
        for top, whole in zip(tops, held[1:]):
            top[:, cols] = whole[:count, cols]


def main_call(value, gate, taps, fwd, inv):
    rows, chans = value.shape
    count = taps.shape[0]
    top = jax.ShapeDtypeStruct((count, chans), jnp.bfloat16)
    return pl.pallas_call(
        main_body,
        in_specs=[IN_HBM] * 5,
        out_specs=[IN_VMEM] * 4,
        out_shape=[
            jax.ShapeDtypeStruct((rows - count, chans), jnp.float32),
            jax.ShapeDtypeStruct((2 * count, chans), jnp.float32),
            top,
            top,
        ],
        scratch_shapes=[
            pltpu.VMEM(taps.shape, taps.dtype),
            pltpu.VMEM(value.shape, value.dtype),
            pltpu.VMEM(gate.shape, gate.dtype),
            pltpu.VMEM(fwd.shape, fwd.dtype),
            pltpu.VMEM(inv.shape, inv.dtype),
            pltpu.SemaphoreType.DMA((1 + chans // (2 * LANES), 3)),
        ],
        compiler_params=kernel_params(16),
        cost_estimate=cost(4),
        name="short_main",
    )(value, gate, taps, fwd, inv)


def head_body(part, count, me, halo, value, gate, gated, taps_spec, long_taps, fwd, inv, *rest):
    taps = halo.shape[0]
    rows = taps + gated.shape[0]
    groups = 8
    outs = rest[-2 * len(part) :]
    tops, codes = outs[: len(part)], outs[len(part) :]
    for d, top, code in zip(part, tops, codes):
        slab = lax.rem(me[0] + d, count)
        cols = lanes_of(slab)
        ext = jnp.concatenate([halo[:, cols], value[:, cols]], 0)
        short = short_rows(ext, taps_spec[:, cols], fwd, inv)
        first = gate[:, cols].astype(jnp.float32) * short
        top[...] = first
        later = gated[:, cols]
        peak = jnp.maximum(
            jnp.max(jnp.abs(first), axis=0, keepdims=True),
            jnp.max(jnp.abs(later), axis=0, keepdims=True),
        )
        scale = scale_of(peak)
        held = long_taps[slab]
        size = jnp.abs(held)
        most = size[:groups]
        for c in range(groups, held.shape[0], groups):
            most = jnp.maximum(most, size[c : c + groups])
        filter_scale = scale_of(jnp.max(most, axis=1, keepdims=True))
        filter_scale = jnp.broadcast_to(filter_scale, (groups, LANES))
        many = held.shape[0] // groups
        code[:taps] = to_code(first, scale)
        code[taps:rows] = to_code(later, scale)
        both = jnp.concatenate([jnp.broadcast_to(scale, (8, LANES)), filter_scale], 0)
        code[rows : rows + TILE] = both.astype(jnp.bfloat16)
        code[rows + TILE :] = to_code(held, jnp.concatenate([filter_scale] * many, 0))


def head_call(part, count, me, halo, value, gate, gated, taps_spec, long_taps, fwd, inv, after):
    taps = halo.shape[0]
    rows = taps + gated.shape[0]
    held = long_taps.shape[1]
    code = jax.ShapeDtypeStruct((rows + TILE + held, LANES), jnp.bfloat16)
    top = jax.ShapeDtypeStruct((taps, LANES), jnp.float32)
    return pl.pallas_call(
        functools.partial(head_body, part, count),
        in_specs=[IN_SMEM] + [IN_VMEM] * 8 + [IN_ANY] * len(after),
        out_specs=[IN_VMEM] * (2 * len(part)),
        out_shape=[top] * len(part) + [code] * len(part),
        compiler_params=kernel_params(12),
        cost_estimate=cost(len(part)),
        name="short_head",
    )(me, halo, value, gate, gated, taps_spec, long_taps, fwd, inv, *after)


def forward_body(code, fwd, turn, widen, *rest):
    spec_out, filter_out, held_x, held_h = rest[-4:]
    rows = held_x.shape[0]
    half = rows // 2
    groups = 8
    held_x[...] = from_code(code[:rows], code[rows : rows + 1].astype(jnp.float32))
    scale = code[rows : rows + TILE].astype(jnp.float32)[groups:]
    taps = code[rows + TILE :]
    many = taps.shape[0] // groups
    h_high, h_low = split(from_code(taps, jnp.concatenate([scale] * many, 0)))
    h_high, h_low = h_high.astype(jnp.float32), h_low.astype(jnp.float32)
    for c in range(many):
        at = slice(c * groups, (c + 1) * groups)
        pair = jnp.concatenate([h_high[at], h_low[at]], 0).T.astype(jnp.bfloat16)
        wide = dot(pair, widen[...])
        for k in range(2):
            held_h[k, c * LANES : (c + 1) * LANES] = wide[:, k * LANES : (k + 1) * LANES]
    highs, lows = [], []
    for odd in range(2):
        step = pl.ds(odd, half, stride=2)
        high, low = split(held_x[step])
        highs += [high, held_h[0, step].astype(jnp.bfloat16)]
        lows += [low, held_h[1, step].astype(jnp.bfloat16)]
    width = 4 * LANES
    both = dot(fwd[0], jnp.concatenate(highs + lows, 1))
    both = both[:, :width] + both[:, width:] + dot(fwd[1], jnp.concatenate(highs, 1))
    w_re, w_im = turn[:half], turn[half:]
    for at, out in enumerate((spec_out, filter_out)):
        even = both[:, at * LANES : (at + 1) * LANES]
        odd = both[:, (2 + at) * LANES : (3 + at) * LANES]
        o_re, o_im = odd[:half], odd[half:]
        t_re = o_re * w_re - o_im * w_im
        t_im = o_re * w_im + o_im * w_re
        out[:half] = even[:half] + t_re
        out[half:rows] = even[:half] - t_re
        out[rows : rows + half] = even[half:] + t_im
        out[rows + half :] = even[half:] - t_im


def forward_call(code, fwd, turn, widen, early, after):
    rows = 2 * fwd.shape[2]
    spec = jax.ShapeDtypeStruct((2 * rows, LANES), jnp.float32)
    return pl.pallas_call(
        forward_body,
        in_specs=[IN_VMEM] * (4 + len(early)) + [IN_ANY] * len(after),
        out_specs=[IN_VMEM] * 2,
        out_shape=[spec, spec],
        scratch_shapes=[
            pltpu.VMEM((rows, LANES), jnp.float32),
            pltpu.VMEM((2, rows, LANES), jnp.float32),
        ],
        compiler_params=kernel_params(12),
        cost_estimate=cost(1),
        name="forward",
    )(code, fwd, turn, widen, *early, *after)


def by_lag_body(me_ref, *refs):
    spectra, out = refs[:-1], refs[-1]
    count = len(spectra)
    half = out.shape[1] // 2
    me = me_ref[0]
    odd = lax.broadcasted_iota(jnp.int32, (8, LANES), 0) % 2 == 1
    sign = jnp.where(odd, 1.0, -1.0)
    lags = [lax.rem(me - d + count, count) for d in range(count)]
    signs = [sign * (lag > 0).astype(jnp.float32) for lag in lags]

    def chunk(c, _):
        re = pl.ds(pl.multiple_of(c * 8, 8), 8)
        im = pl.ds(pl.multiple_of(half + c * 8, 8), 8)
        for d in range(count):
            before = spectra[(d + 1) % count]
            out[lags[d], re] = spectra[d][re] + signs[d] * before[im]
            out[lags[d], im] = spectra[d][im] - signs[d] * before[re]
        out[count, re] = jnp.zeros((8, LANES), jnp.float32)
        out[count, im] = jnp.zeros((8, LANES), jnp.float32)
        return 0

    lax.fori_loop(0, half // 8, chunk, 0, unroll=2)


def by_lag_call(me, spectra):
    count = len(spectra)
    bins = spectra[0].shape[0]
    return pl.pallas_call(
        by_lag_body,
        in_specs=[IN_SMEM] + [IN_VMEM] * count,
        out_specs=IN_VMEM,
        out_shape=jax.ShapeDtypeStruct((count + 1, bins, LANES), jnp.float32),
        compiler_params=kernel_params(12),
        cost_estimate=cost(1),
        name="by_lag",
    )(me, *spectra)


def back_body(part, count, me_ref, filt, inv, turn, *refs):
    specs, codes, total, held = refs[:count], refs[-2 - len(part) : -2], refs[-2], refs[-1]
    rows = held.shape[0]
    half = rows // 2
    me = me_ref[0]

    for e, code in zip(part, codes):
        target = lax.rem(me + e, count)
        lags = []
        for d in range(count):
            lag = target - lax.rem(me - d + count, count)
            lags.append(jnp.where(lag >= 0, lag, count))

        def chunk(c, _):
            def piece(start):
                return pl.ds(pl.multiple_of(start + c * 8, 8), 8)

            sums = []
            for start in (0, half):
                re, im = piece(start), piece(rows + start)
                acc_re = jnp.zeros((8, LANES), jnp.float32)
                acc_im = acc_re
                for d in range(count):
                    x_re, x_im = specs[d][re], specs[d][im]
                    g_re, g_im = filt[lags[d], re], filt[lags[d], im]
                    acc_re += x_re * g_re - x_im * g_im
                    acc_im += x_re * g_im + x_im * g_re
                sums += [acc_re, acc_im]
            a_re, a_im, b_re, b_im = sums
            re, im = piece(0), piece(half)
            w_re, w_im = turn[re], turn[im]
            d_re, d_im = a_re - b_re, a_im - b_im
            total[re, :LANES] = a_re + b_re
            total[im, :LANES] = a_im + b_im
            total[re, LANES:] = d_re * w_re + d_im * w_im
            total[im, LANES:] = d_im * w_re - d_re * w_im
            return 0

        lax.fori_loop(0, half // 8, chunk, 0, unroll=2)
        values = dot3(inv, total[...])
        held[pl.ds(0, half, stride=2)] = values[:, :LANES]
        held[pl.ds(1, half, stride=2)] = values[:, LANES:]
        peak = jnp.max(jnp.abs(values), axis=0, keepdims=True)
        scale = scale_of(jnp.maximum(peak[:, :LANES], peak[:, LANES:]))
        code[:rows] = to_code(held[...], scale)
        code[rows:] = jnp.broadcast_to(scale, (TILE, LANES)).astype(jnp.bfloat16)


def back_call(part, me, filt, inv, turn, specs, after):
    count = len(specs)
    bins = specs[0].shape[0]
    code = jax.ShapeDtypeStruct((bins // 2 + TILE, LANES), jnp.bfloat16)
    return pl.pallas_call(
        functools.partial(back_body, part, count),
        in_specs=[IN_SMEM] + [IN_VMEM] * (3 + count) + [IN_ANY] * len(after),
        out_specs=[IN_VMEM] * len(part),
        out_shape=[code] * len(part),
        scratch_shapes=[
            pltpu.VMEM((bins // 2, 2 * LANES), jnp.float32),
            pltpu.VMEM((bins // 2, LANES), jnp.float32),
        ],
        compiler_params=kernel_params(12),
        cost_estimate=cost(len(part)),
        name="back",
    )(me, filt, inv, turn, *specs, *after)


def final_body(part, count, me, *refs):
    many = len(part)
    codes, tops, (gated, gate, skip) = refs[:many], refs[many : 2 * many], refs[2 * many : 2 * many + 3]
    out, held, sems = refs[-3:]
    taps = tops[0].shape[0]
    rows = gate.shape[0]
    copies = []
    for at, d in enumerate(part):
        cols = lanes_of(lax.rem(me[0] + d, count))
        code, top = codes[at], tops[at]
        scale = code[rows : rows + 1].astype(jnp.float32)
        for r, part_gated in ((slice(0, taps), top[...]), (slice(taps, rows), gated[:, cols])):
            total = from_code(code[r], scale) + skip[:, cols] * part_gated
            held[at, r] = (gate[r, cols].astype(jnp.float32) * total).astype(jnp.bfloat16)
        copies.append(pltpu.make_async_copy(held.at[at], out.at[:, cols], sems.at[at]))
        copies[-1].start()
    for copy in copies:
        copy.wait()


def final_call(part, count, me, codes, tops, gated, gate, skip, so_far, after):
    rows = gate.shape[0]
    many = len(part)
    args = [me, *codes, *tops, gated, gate, skip]
    specs = [IN_SMEM] + [IN_VMEM] * (2 * many + 3)
    alias = {}
    if so_far:
        alias = {len(args): 0}
    args += so_far + after
    specs += [IN_ANY] * len(so_far + after)
    return pl.pallas_call(
        functools.partial(final_body, part, count),
        in_specs=specs,
        out_specs=IN_ANY,
        out_shape=jax.ShapeDtypeStruct(gate.shape, jnp.bfloat16),
        scratch_shapes=[
            pltpu.VMEM((many, rows, LANES), jnp.bfloat16),
            pltpu.SemaphoreType.DMA((many,)),
        ],
        input_output_aliases=alias,
        compiler_params=kernel_params(12),
        cost_estimate=cost(many),
        name="final",
    )(*args)


def rotation_order(count):
    return sorted(range(1, count), key=lambda d: (-min(d, count - d), d))


def in_slabs(output_gate, input_gate, value_input, short_filter, long_filter, skip_gain):
    count = lax.axis_size("ctx")
    me = lax.axis_index("ctx").reshape(1)
    rows = value_input.shape[0]
    taps = short_filter.shape[0]
    groups = long_filter.shape[1] // count
    order = rotation_order(count) + [0]

    def rotated(block, distance):
        return lax.ppermute(block, "ctx", [(i, (i + distance) % count) for i in range(count)])

    def table(values):
        return jnp.asarray(split_table(values))

    halo = passed_along(tail_call(value_input, taps), "ctx", 1)
    long_taps = long_filter.T.reshape(count, groups, rows // LANES, LANES)
    long_taps = jnp.swapaxes(long_taps, 1, 2).reshape(count, -1, LANES)

    forward, inverse = tables(taps)
    short_fwd, short_inv = table(forward), table(inverse[taps:])
    half = rows // 2
    forward, inverse = tables(half)
    fwd, inv = table(forward[:, :half]), table(inverse[:half] / 2)
    turn = jnp.asarray(turning(rows, LANES))
    widen = jnp.asarray(widening(groups, LANES))

    gated, taps_spec, value_top, gate_top = main_call(
        value_input, input_gate, short_filter, short_fwd, short_inv
    )
    came, tops, codes, specs, spectra = {}, {}, {}, {}, {}
    after = []

    def heads(*part):
        outs = head_call(
            part, count, me, halo, value_top, gate_top, gated, taps_spec, long_taps,
            short_fwd, short_inv, after,
        )
        after[:] = outs[:1]
        for d, top, code in zip(part, outs, outs[len(part) :]):
            tops[d] = top
            came[d] = rotated(code, d) if d else code

    def forwards(d, early=()):
        specs[d], spectra[d] = forward_call(came[d], fwd, turn, widen, early, after)
        after[:] = [specs[d]]

    heads(order[0])
    heads(*order[1:3])
    heads(*order[3:5], 0)
    forwards(0, [inv])
    forwards(order[0])
    heads(order[5])
    forwards(order[1])
    heads(order[6])
    for d in order[2:7]:
        forwards(d)
    specs = [specs[d] for d in range(count)]
    filt = by_lag_call(me, [spectra[d] for d in range(count)])

    answers, after = {}, []
    mixed = []

    def backs(e):
        (code,) = back_call([e], me, filt, inv, turn, specs, after)
        answers[e] = rotated(code, e) if e else code
        after[:] = [code]

    def finals(*part):
        owners = [(count - e) % count for e in part]
        mixed[:] = [
            final_call(
                owners, count, me, [answers[e] for e in part], [tops[d] for d in owners],
                gated, output_gate, skip_gain[None], mixed, after,
            )
        ]
        after[:] = mixed

    for e in order[:5]:
        backs(e)
    backs(0)
    finals(0, order[0])
    backs(order[5])
    finals(order[1])
    backs(order[6])
    for e in order[2:7]:
        finals(e)
    return mixed[0]


def local(output_gate, input_gate, value_input, short_filter, long_filter, skip_gain):
    count = lax.axis_size("ctx")
    rows, chans = value_input.shape
    taps = short_filter.shape[0]
    groups = long_filter.shape[1]
    fits = chans == LANES * count and groups == 8 * count and taps == LANES
    fits = fits and rows % taps == 0 and rows > taps
    run = in_slabs if fits else plain
    return run(output_gate, input_gate, value_input, short_filter, long_filter, skip_gain)


def solution(mesh):
    placed = (
        P("ctx", "ch"),
        P("ctx", "ch"),
        P("ctx", "ch"),
        P(None, "ch"),
        P("ctx", "ch"),
        P("ch"),
    )
    return jax.shard_map(
        local, mesh=mesh, in_specs=placed, out_specs=P("ctx", "ch"), check_vma=False
    )
```

```python
import functools
import math

import jax
import jax.numpy as jnp
import numpy as np
from jax import lax
from jax.experimental import pallas as pl
from jax.experimental.pallas import tpu as pltpu
from jax.sharding import PartitionSpec as P

HIGHEST = lax.Precision.HIGHEST
LANES = 128
TILE = 16
SPAN = 250.0
BIAS = 125.0
TINY = 1e-30
MIB = 1 << 20


def passed_along(block, axis, distance):
    devices = range(lax.axis_size(axis))
    route = [(i - distance, i) for i in devices if i - distance in devices]
    return lax.ppermute(block, axis, route)


def depthwise(extended, filter_taps):
    kernel = filter_taps[::-1][:, None, :]
    result = lax.conv_general_dilated(
        extended[None],
        kernel,
        (1,),
        "VALID",
        dimension_numbers=("NWC", "WIO", "NWC"),
        feature_group_count=extended.shape[1],
        precision=HIGHEST,
    )
    return result[0]


def rotate(real_part, imag_part, cosine, sine):
    return (real_part * cosine - imag_part * sine, real_part * sine + imag_part * cosine)


def table_apply(pattern, cosine, sine, real_part, imag_part):
    out_real = jnp.einsum(pattern, cosine, real_part, precision=HIGHEST) - jnp.einsum(
        pattern, sine, imag_part, precision=HIGHEST
    )
    out_imag = jnp.einsum(pattern, cosine, imag_part, precision=HIGHEST) + jnp.einsum(
        pattern, sine, real_part, precision=HIGHEST
    )
    return (out_real, out_imag)


def dft_table(length, sign):
    index_vals = jnp.arange(length, dtype=jnp.int32)
    exponent = index_vals[:, None] * index_vals[None, :] % length
    angle = sign * 2.0 * math.pi * exponent.astype(jnp.float32) / length
    return (jnp.cos(angle), jnp.sin(angle))


def channel_local(signal, filt):
    length, cols = signal.shape
    fft_length = 2 * length
    size_a = math.gcd(length, 1 << fft_length.bit_length() // 2)
    size_b = fft_length // size_a
    half_b = size_b // 2
    pair_cols = cols // 2
    paired = signal.reshape(half_b, size_a, pair_cols, 2)
    sig_real = paired[..., 0]
    sig_imag = paired[..., 1]
    filt_real = filt.reshape(half_b, size_a, pair_cols, 2)[..., 0]
    b_cos, b_sin = dft_table(size_b, -1.0)
    in_cos = b_cos[:, :half_b]
    in_sin = b_sin[:, :half_b]
    data_real, data_imag = table_apply("kb,bap->kap", in_cos, in_sin, sig_real, sig_imag)
    spec_real = jnp.einsum("kb,bap->kap", in_cos, filt_real, precision=HIGHEST)
    spec_imag = jnp.einsum("kb,bap->kap", in_sin, filt_real, precision=HIGHEST)
    fine_index = jnp.arange(size_b, dtype=jnp.int32)
    coarse_index = jnp.arange(size_a, dtype=jnp.int32)
    exponent = fine_index[:, None] * coarse_index[None, :] % fft_length
    tw_angle = -2.0 * math.pi * exponent.astype(jnp.float32) / fft_length
    tw_cos = jnp.cos(tw_angle)[:, :, None]
    tw_sin = jnp.sin(tw_angle)[:, :, None]
    data_real, data_imag = rotate(data_real, data_imag, tw_cos, tw_sin)
    spec_real, spec_imag = rotate(spec_real, spec_imag, tw_cos, tw_sin)
    a_cos, a_sin = dft_table(size_a, -1.0)
    data_real, data_imag = table_apply("ka,bap->bkp", a_cos, a_sin, data_real, data_imag)
    spec_real, spec_imag = table_apply("ka,bap->bkp", a_cos, a_sin, spec_real, spec_imag)
    prod_real = data_real * spec_real - data_imag * spec_imag
    prod_imag = data_real * spec_imag + data_imag * spec_real
    back_real, back_imag = table_apply("ak,bkp->bap", a_cos, -a_sin, prod_real, prod_imag)
    back_real, back_imag = rotate(back_real, back_imag, tw_cos, -tw_sin)
    final_real, final_imag = table_apply(
        "bk,kap->bap", b_cos[:half_b], -b_sin[:half_b], back_real, back_imag
    )
    joined = jnp.stack([final_real, final_imag], axis=-1).reshape(length, cols)
    return joined / fft_length


def plain(output_gate, input_gate, value_input, short_filter, long_filter, skip_gain):
    row_count, chan_count = value_input.shape
    group_total = long_filter.shape[1]
    tap_count = short_filter.shape[0]
    earlier = passed_along(value_input[row_count - tap_count + 1 :], "ctx", 1)
    extended = jnp.concatenate([earlier, value_input], axis=0).astype(jnp.float32)
    gated = input_gate.astype(jnp.float32) * depthwise(extended, short_filter)
    widened = jnp.repeat(long_filter, chan_count // group_total, axis=1)
    moved = (
        lax.all_to_all(gated, "ctx", split_axis=1, concat_axis=0, tiled=True),
        lax.all_to_all(widened, "ctx", split_axis=1, concat_axis=0, tiled=True),
    )
    convolved = channel_local(moved[0], moved[1])
    long_out = lax.all_to_all(convolved, "ctx", split_axis=0, concat_axis=1, tiled=True)
    mixed = output_gate.astype(jnp.float32) * (long_out + skip_gain[None, :] * gated)
    return mixed.astype(jnp.bfloat16)


def split(values):
    high = values.astype(jnp.bfloat16)
    return high, (values - high.astype(jnp.float32)).astype(jnp.bfloat16)


def split_table(table):
    high = table.astype(np.float32).astype(jnp.bfloat16)
    low = (table - high.astype(np.float64)).astype(np.float32).astype(jnp.bfloat16)
    return np.stack([high, low])


@functools.lru_cache
def tables(half):
    bins = np.arange(half)[:, None] + 0.5
    angle = 2.0 * np.pi * bins * np.arange(2 * half)[None, :] / (2 * half)
    forward = np.concatenate([np.cos(angle), -np.sin(angle)], 0)
    return forward, forward.T / half


def turning(rows, lanes):
    angle = 2.0 * np.pi * (np.arange(rows // 2) + 0.5) / (2 * rows)
    both = np.concatenate([np.cos(angle), -np.sin(angle)]).astype(np.float32)
    return np.repeat(both[:, None], lanes, 1)


def widening(groups, lanes):
    one = np.kron(np.eye(groups), np.ones((1, lanes // groups)))
    return np.kron(np.eye(2), one).astype(jnp.bfloat16)


def dot(a, b):
    return jnp.dot(a, b, preferred_element_type=jnp.float32)


def dot3(table, values):
    high, low = split(values)
    cols = values.shape[1]
    both = dot(table[0], jnp.concatenate([high, low], 1))
    return both[:, :cols] + both[:, cols:] + dot(table[1], high)


def scale_of(top):
    return jnp.maximum(top * 1.01, TINY).astype(jnp.bfloat16).astype(jnp.float32)


def to_code(values, scale):
    power = jnp.exp2(jnp.abs(values) * (SPAN / scale) - BIAS)
    return jnp.where(values < 0.0, -power, power).astype(jnp.bfloat16)


def from_code(code, scale):
    power = code.astype(jnp.float32)
    size = (jnp.log(jnp.abs(power)) * (1.0 / math.log(2.0)) + BIAS) * (scale * (1.0 / SPAN))
    return jnp.where(power < 0.0, -size, size)


def short_rows(ext, taps_spec, fwd, inv):
    count = taps_spec.shape[0] // 2
    rows, cols = ext.shape
    starts = range(0, rows - count, count)
    wide = jnp.concatenate([ext[s : s + 2 * count] for s in starts], 1)
    spec = dot(fwd[0], wide) + dot(fwd[1], wide)
    t_re = jnp.concatenate([taps_spec[:count]] * len(starts), 1)
    t_im = jnp.concatenate([taps_spec[count:]] * len(starts), 1)
    s_re, s_im = spec[:count], spec[count:]
    prod = jnp.concatenate([s_re * t_re - s_im * t_im, s_re * t_im + s_im * t_re], 0)
    back = dot3(inv, prod)
    return jnp.concatenate([back[:, w * cols : (w + 1) * cols] for w in range(len(starts))], 0)


IN_VMEM = pl.BlockSpec(memory_space=pltpu.VMEM)
IN_SMEM = pl.BlockSpec(memory_space=pltpu.SMEM)
IN_ANY = pl.BlockSpec(memory_space=pl.ANY)
IN_HBM = pl.BlockSpec(memory_space=pltpu.HBM)


def kernel_params(mib):
    return pltpu.CompilerParams(vmem_limit_bytes=mib * MIB)


def cost(scale):
    return pl.CostEstimate(flops=0, bytes_accessed=0, transcendentals=0)


def lanes_of(slab):
    return pl.ds(pl.multiple_of(slab * LANES, LANES), LANES)


def pace_body(me, out):
    out[0] = me[0]


def pace_call(me):
    return pl.pallas_call(
        pace_body,
        in_specs=[IN_SMEM],
        out_specs=IN_SMEM,
        out_shape=jax.ShapeDtypeStruct((1,), jnp.int32),
        compiler_params=kernel_params(4),
        cost_estimate=pl.CostEstimate(flops=10_000_000_000, bytes_accessed=8, transcendentals=0),
        name="pace",
    )(me)


def main_body(me, value, gate, taps, fwd, inv, gated, spec_out):
    count = taps.shape[0]
    wide = 2 * LANES
    for c in range(0, value.shape[1], wide):
        cols = slice(c, c + wide)
        taps_spec = dot3(fwd[:, :, :count], taps[:, cols])
        spec_out[:, cols] = taps_spec
        short = short_rows(value[:, cols], taps_spec, fwd, inv)
        gated[:, cols] = gate[count:, cols].astype(jnp.float32) * short


def main_call(me, value, gate, taps, fwd, inv, after):
    rows, chans = value.shape
    count = taps.shape[0]
    return pl.pallas_call(
        drop_after(main_body, 6, len(after)),
        in_specs=[IN_SMEM] + [IN_VMEM] * 5 + [IN_ANY] * len(after),
        out_specs=[IN_VMEM] * 2,
        out_shape=[
            jax.ShapeDtypeStruct((rows - count, chans), jnp.float32),
            jax.ShapeDtypeStruct((2 * count, chans), jnp.float32),
        ],
        compiler_params=kernel_params(12),
        cost_estimate=cost(4),
        name="short_main",
    )(me, value, gate, taps, fwd, inv, *after)


def drop_after(body, keep, unused):
    return lambda *refs: body(*refs[:keep], *refs[keep + unused :])


def write_code(code, values, filter_rows):
    groups = 8
    rows = sum(v.shape[0] for v in values)
    peak = functools.reduce(
        jnp.maximum, [jnp.max(jnp.abs(v), axis=0, keepdims=True) for v in values]
    )
    scale = scale_of(peak)
    start = 0
    for v in values:
        code[start : start + v.shape[0]] = to_code(v, scale)
        start += v.shape[0]
    scale = jnp.broadcast_to(scale, (groups, LANES))
    if filter_rows is None:
        both = jnp.concatenate([scale, scale], 0)
    else:
        size = jnp.abs(filter_rows)
        many = filter_rows.shape[0] // groups
        most = size[:groups]
        for c in range(1, many):
            most = jnp.maximum(most, size[c * groups : (c + 1) * groups])
        filter_scale = scale_of(jnp.max(most, axis=1, keepdims=True))
        filter_scale = jnp.broadcast_to(filter_scale, (groups, LANES))
        both = jnp.concatenate([scale, filter_scale], 0)
        code[rows + TILE :] = to_code(filter_rows, jnp.concatenate([filter_scale] * many, 0))
    code[rows : rows + TILE] = both.astype(jnp.bfloat16)


def ahead_body(part, me, value, gate, taps, long_taps, fwd, inv, *codes):
    count = taps.shape[0]
    for d, code in zip(part, codes):
        slab = me[0] ^ d
        cols = lanes_of(slab)
        taps_spec = dot3(fwd[:, :, :count], taps[:, cols])
        short = short_rows(value[:, cols], taps_spec, fwd, inv)
        write_code(code, [gate[count:, cols].astype(jnp.float32) * short], long_taps[slab])


def ahead_call(part, me, value, gate, taps, long_taps, fwd, inv, after):
    rows = value.shape[0] - taps.shape[0] + TILE + long_taps.shape[1]
    code = jax.ShapeDtypeStruct((rows, LANES), jnp.bfloat16)
    return pl.pallas_call(
        drop_after(functools.partial(ahead_body, part), 7, len(after)),
        in_specs=[IN_SMEM] + [IN_VMEM] * 6 + [IN_ANY] * len(after),
        out_specs=[IN_VMEM] * len(part),
        out_shape=[code] * len(part),
        compiler_params=kernel_params(12),
        cost_estimate=cost(1),
        name="short_ahead",
    )(me, value, gate, taps, long_taps, fwd, inv, *after)


def head_body(part, ahead, me, halo, value, gate, gated, taps_spec, long_taps, fwd, inv, *outs):
    taps = halo.shape[0]
    tops, codes = outs[: len(part)], outs[len(part) :]
    for d, top, code in zip(part, tops, codes):
        slab = me[0] ^ d
        cols = lanes_of(slab)
        ext = jnp.concatenate([halo[:, cols], value[:taps, cols]], 0)
        short = short_rows(ext, taps_spec[:, cols], fwd, inv)
        first = gate[:taps, cols].astype(jnp.float32) * short
        top[...] = first
        if d in ahead:
            write_code(code, [first], None)
        else:
            write_code(code, [first, gated[:, cols]], long_taps[slab])


def head_call(part, ahead, me, halo, value, gate, gated, taps_spec, long_taps, fwd, inv, after):
    taps = halo.shape[0]
    whole = taps + gated.shape[0] + TILE + long_taps.shape[1]
    codes = [
        jax.ShapeDtypeStruct((taps + TILE if d in ahead else whole, LANES), jnp.bfloat16)
        for d in part
    ]
    top = jax.ShapeDtypeStruct((taps, LANES), jnp.float32)
    return pl.pallas_call(
        drop_after(functools.partial(head_body, part, ahead), 9, len(after)),
        in_specs=[IN_SMEM] + [IN_VMEM] * 8 + [IN_ANY] * len(after),
        out_specs=[IN_VMEM] * (2 * len(part)),
        out_shape=[top] * len(part) + codes,
        compiler_params=kernel_params(12),
        cost_estimate=cost(len(part)),
        name="short_head",
    )(me, halo, value, gate, gated, taps_spec, long_taps, fwd, inv, *after)


def forward_body(d, clear, pieces, me, fwd, turn, widen, *rest):
    spec_out, filter_out, held_x, held_h = rest[-4:]
    rows = held_x.shape[0]
    half = rows // 2
    groups = 8
    end = rows
    for code, length in zip(rest, pieces):
        scales = code[length : length + TILE].astype(jnp.float32)
        held_x[end - length : end] = from_code(code[:length], scales[:1])
        end -= length
    code, length = rest[0], pieces[0]
    scale = code[length : length + TILE].astype(jnp.float32)[groups:]
    taps = code[length + TILE :]
    many = taps.shape[0] // groups
    h_high, h_low = split(from_code(taps, jnp.concatenate([scale] * many, 0)))
    h_high, h_low = h_high.astype(jnp.float32), h_low.astype(jnp.float32)
    for c in range(many):
        at = slice(c * groups, (c + 1) * groups)
        pair = jnp.concatenate([h_high[at], h_low[at]], 0).T.astype(jnp.bfloat16)
        wide = dot(pair, widen[...])
        for k in range(2):
            held_h[k, c * LANES : (c + 1) * LANES] = wide[:, k * LANES : (k + 1) * LANES]
    highs, lows = [], []
    for odd in range(2):
        step = pl.ds(odd, half, stride=2)
        high, low = split(held_x[step])
        highs += [high, held_h[0, step].astype(jnp.bfloat16)]
        lows += [low, held_h[1, step].astype(jnp.bfloat16)]
    width = 4 * LANES
    both = dot(fwd[0], jnp.concatenate(highs + lows, 1))
    both = both[:, :width] + both[:, width:] + dot(fwd[1], jnp.concatenate(highs, 1))
    w_re, w_im = turn[:half], turn[half:]
    outs = []
    for at in range(2):
        even = both[:, at * LANES : (at + 1) * LANES]
        odd = both[:, (2 + at) * LANES : (3 + at) * LANES]
        o_re, o_im = odd[:half], odd[half:]
        t_re = o_re * w_re - o_im * w_im
        t_im = o_re * w_im + o_im * w_re
        outs.append((even[:half] + t_re, even[:half] - t_re, even[half:] + t_im, even[half:] - t_im))
    for c, piece in enumerate(outs[0]):
        spec_out[c * half : (c + 1) * half] = piece
    if clear:
        filter_out[...] = jnp.zeros_like(filter_out)
    own = me[0] ^ d
    later = jnp.where(own + 1 < filter_out.shape[0] - 2, own + 1, own + 2)
    odd = lax.broadcasted_iota(jnp.int32, (half, LANES), 0) % 2 == 1
    for c, piece in enumerate(outs[1]):
        filter_out[own, c * half : (c + 1) * half] += piece
        moved = jnp.where(odd, -piece, piece) if c < 2 else jnp.where(odd, piece, -piece)
        at = slice(((c + 2) % 4) * half, ((c + 2) % 4 + 1) * half)
        filter_out[later, at] += moved


def forward_call(d, count, me, codes, fwd, turn, widen, early, so_far, after):
    rows = 2 * fwd.shape[2]
    held = so_far + early
    last = codes[-1].shape[0] - TILE
    pieces = [rows - last, last] if len(codes) > 1 else [rows]
    return pl.pallas_call(
        functools.partial(forward_body, d, not so_far, pieces),
        in_specs=[IN_SMEM] + [IN_VMEM] * (3 + len(codes) + len(held)) + [IN_ANY] * len(after),
        out_specs=[IN_VMEM] * 2,
        out_shape=[
            jax.ShapeDtypeStruct((2 * rows, LANES), jnp.float32),
            jax.ShapeDtypeStruct((count + 2, 2 * rows, LANES), jnp.float32),
        ],
        scratch_shapes=[
            pltpu.VMEM((rows, LANES), jnp.float32),
            pltpu.VMEM((2, rows, LANES), jnp.float32),
        ],
        input_output_aliases={4 + len(codes): 1} if so_far else {},
        compiler_params=kernel_params(12),
        cost_estimate=cost(1),
        name="forward",
    )(me, fwd, turn, widen, *codes, *held, *after)


def back_body(part, count, me_ref, filt, inv, turn, *refs):
    specs, codes, total, held = refs[:count], refs[-2 - len(part) : -2], refs[-2], refs[-1]
    rows = held.shape[0]
    half = rows // 2
    me = me_ref[0]

    for e, code in zip(part, codes):
        lags = []
        for d in range(count):
            lag = (me ^ e) - (me ^ d)
            lags.append(jnp.where(lag >= 0, lag, count))

        def chunk(c, _):
            def piece(start):
                return pl.ds(pl.multiple_of(start + c * 8, 8), 8)

            sums = []
            for start in (0, half):
                re, im = piece(start), piece(rows + start)
                acc_re = jnp.zeros((8, LANES), jnp.float32)
                acc_im = acc_re
                for d in range(count):
                    x_re, x_im = specs[d][re], specs[d][im]
                    g_re, g_im = filt[lags[d], re], filt[lags[d], im]
                    acc_re += x_re * g_re - x_im * g_im
                    acc_im += x_re * g_im + x_im * g_re
                sums += [acc_re, acc_im]
            a_re, a_im, b_re, b_im = sums
            re, im = piece(0), piece(half)
            w_re, w_im = turn[re], turn[im]
            d_re, d_im = a_re - b_re, a_im - b_im
            total[re, :LANES] = a_re + b_re
            total[im, :LANES] = a_im + b_im
            total[re, LANES:] = d_re * w_re + d_im * w_im
            total[im, LANES:] = d_im * w_re - d_re * w_im
            return 0

        lax.fori_loop(0, half // 8, chunk, 0, unroll=4)
        values = dot3(inv, total[...])
        held[pl.ds(0, half, stride=2)] = values[:, :LANES]
        held[pl.ds(1, half, stride=2)] = values[:, LANES:]
        peak = jnp.max(jnp.abs(values), axis=0, keepdims=True)
        scale = scale_of(jnp.maximum(peak[:, :LANES], peak[:, LANES:]))
        code[:rows] = to_code(held[...], scale)
        code[rows:] = jnp.broadcast_to(scale, (TILE, LANES)).astype(jnp.bfloat16)


def back_call(part, me, filt, inv, turn, specs, after):
    count = len(specs)
    bins = specs[0].shape[0]
    code = jax.ShapeDtypeStruct((bins // 2 + TILE, LANES), jnp.bfloat16)
    return pl.pallas_call(
        functools.partial(back_body, part, count),
        in_specs=[IN_SMEM] + [IN_VMEM] * (3 + count) + [IN_ANY] * len(after),
        out_specs=[IN_VMEM] * len(part),
        out_shape=[code] * len(part),
        scratch_shapes=[
            pltpu.VMEM((bins // 2, 2 * LANES), jnp.float32),
            pltpu.VMEM((bins // 2, LANES), jnp.float32),
        ],
        compiler_params=kernel_params(12),
        cost_estimate=cost(len(part)),
        name="back",
    )(me, filt, inv, turn, *specs, *after)


def final_body(part, count, me, *refs):
    many = len(part)
    codes, tops, (gated, gate, skip) = refs[:many], refs[many : 2 * many], refs[2 * many : 2 * many + 3]
    out, held, sems = refs[-3:]
    taps = tops[0].shape[0]
    rows = gate.shape[0]
    copies = []
    for at, d in enumerate(part):
        cols = lanes_of(me[0] ^ d)
        code, top = codes[at], tops[at]
        scale = code[rows : rows + 1].astype(jnp.float32)
        for r, part_gated in ((slice(0, taps), top[...]), (slice(taps, rows), gated[:, cols])):
            total = from_code(code[r], scale) + skip[:, cols] * part_gated
            held[at, r] = (gate[r, cols].astype(jnp.float32) * total).astype(jnp.bfloat16)
        copies.append(pltpu.make_async_copy(held.at[at], out.at[:, cols], sems.at[at]))
        copies[-1].start()
    for copy in copies:
        copy.wait()


def final_call(part, count, me, codes, tops, gated, gate, skip, so_far, after):
    rows = gate.shape[0]
    many = len(part)
    args = [me, *codes, *tops, gated, gate, skip]
    specs = [IN_SMEM] + [IN_VMEM] * (2 * many + 3)
    alias = {}
    if so_far:
        alias = {len(args): 0}
    args += so_far + after
    specs += [IN_ANY] * len(so_far + after)
    return pl.pallas_call(
        functools.partial(final_body, part, count),
        in_specs=specs,
        out_specs=IN_ANY,
        out_shape=jax.ShapeDtypeStruct(gate.shape, jnp.bfloat16),
        scratch_shapes=[
            pltpu.VMEM((many, rows, LANES), jnp.bfloat16),
            pltpu.SemaphoreType.DMA((many,)),
        ],
        input_output_aliases=alias,
        compiler_params=kernel_params(12),
        cost_estimate=cost(many),
        name="final",
    )(*args)


def in_slabs(output_gate, input_gate, value_input, short_filter, long_filter, skip_gain):
    count = lax.axis_size("ctx")
    me = lax.axis_index("ctx").reshape(1)
    rows = value_input.shape[0]
    taps = short_filter.shape[0]
    groups = long_filter.shape[1] // count

    def exchanged(block, d):
        return lax.ppermute(block, "ctx", [(i, i ^ d) for i in range(count)]) if d else block

    def table(values):
        return jnp.asarray(split_table(values))

    halo = passed_along(value_input[rows - taps :], "ctx", 1)
    long_taps = long_filter.T.reshape(count, groups, rows // LANES, LANES)
    long_taps = jnp.swapaxes(long_taps, 1, 2).reshape(count, -1, LANES)

    forward, inverse = tables(taps)
    short_fwd, short_inv = table(forward), table(inverse[taps:])
    half = rows // 2
    forward, inverse = tables(half)
    fwd, inv = table(forward[:, :half]), table(inverse[:half] / 2)
    turn = jnp.asarray(turning(rows, LANES))
    widen = jnp.asarray(widening(groups, LANES))

    came, tops, specs, answers = {}, {}, {}, {}
    after, filt, mixed = [], [], []

    paced = pace_call(me)
    main_out = []

    def mains():
        main_out[:] = main_call(
            paced, value_input, input_gate, short_filter, short_fwd, short_inv, after
        )
        after[:] = main_out[:1]

    def aheads(*part):
        codes = ahead_call(
            part, paced, value_input, input_gate, short_filter, long_taps, short_fwd, short_inv,
            after,
        )
        after[:] = codes[:1]
        for d, code in zip(part, codes):
            came[d] = [exchanged(code, d)]

    def heads(*part):
        outs = head_call(
            part, tuple(came), me, halo, value_input, input_gate, *main_out, long_taps,
            short_fwd, short_inv, after,
        )
        after[:] = outs[:1]
        for d, top, code in zip(part, outs, outs[len(part) :]):
            tops[d] = top
            came[d] = came.get(d, []) + [exchanged(code, d)]

    def forwards(*part):
        for d in part:
            specs[d], filt[:] = (lambda a, b: (a, [b]))(
                *forward_call(
                    d, count, me, came[d], fwd, turn, widen, [] if d else [inv], filt, after
                )
            )
            after[:] = [specs[d]]

    def backs(*part):
        held = [specs[d] for d in range(count)]
        for e in part:
            (code,) = back_call([e], me, filt[0], inv, turn, held, after)
            answers[e] = exchanged(code, e)
            after[:] = [code]

    def finals(*part):
        mixed[:] = [
            final_call(
                part, count, me, [answers[e] for e in part], [tops[e] for e in part],
                main_out[0], output_gate, skip_gain[None], mixed, after,
            )
        ]
        after[:] = mixed

    mains()
    heads(4)
    heads(2)
    heads(3)
    heads(5)
    heads(6, 0)
    forwards(0)
    forwards(4)
    heads(1)
    forwards(2)
    heads(7)
    forwards(3)
    forwards(5)
    forwards(6)
    forwards(1)
    forwards(7)
    backs(4)
    backs(5)
    backs(6)
    backs(7)
    backs(3)
    backs(0)
    finals(0, 4)
    backs(2)
    finals(5)
    backs(1)
    finals(6, 7)
    finals(3)
    finals(2)
    finals(1)
    return mixed[0]


def local(output_gate, input_gate, value_input, short_filter, long_filter, skip_gain):
    count = lax.axis_size("ctx")
    rows, chans = value_input.shape
    taps = short_filter.shape[0]
    groups = long_filter.shape[1]
    fits = chans == LANES * count and groups == 8 * count and taps == LANES
    fits = fits and rows % taps == 0 and rows > taps
    run = in_slabs if fits else plain
    return run(output_gate, input_gate, value_input, short_filter, long_filter, skip_gain)


def solution(mesh):
    placed = (
        P("ctx", "ch"),
        P("ctx", "ch"),
        P("ctx", "ch"),
        P(None, "ch"),
        P("ctx", "ch"),
        P("ch"),
    )
    return jax.shard_map(
        local, mesh=mesh, in_specs=placed, out_specs=P("ctx", "ch"), check_vma=False
    )
```

```python
import functools
import math

import jax
import jax.numpy as jnp
import numpy as np
from jax import lax
from jax.experimental import pallas as pl
from jax.experimental.pallas import tpu as pltpu
from jax.sharding import PartitionSpec as P

HIGHEST = lax.Precision.HIGHEST
LANES = 128
TILE = 8
SPAN = 250.0
BIAS = 125.0
TINY = 1e-30
MIB = 1 << 20


def passed_along(block, axis, distance):
    devices = range(lax.axis_size(axis))
    route = [(i - distance, i) for i in devices if i - distance in devices]
    return lax.ppermute(block, axis, route)


def depthwise(extended, filter_taps):
    kernel = filter_taps[::-1][:, None, :]
    result = lax.conv_general_dilated(
        extended[None],
        kernel,
        (1,),
        "VALID",
        dimension_numbers=("NWC", "WIO", "NWC"),
        feature_group_count=extended.shape[1],
        precision=HIGHEST,
    )
    return result[0]


def rotate(real_part, imag_part, cosine, sine):
    return (real_part * cosine - imag_part * sine, real_part * sine + imag_part * cosine)


def table_apply(pattern, cosine, sine, real_part, imag_part):
    out_real = jnp.einsum(pattern, cosine, real_part, precision=HIGHEST) - jnp.einsum(
        pattern, sine, imag_part, precision=HIGHEST
    )
    out_imag = jnp.einsum(pattern, cosine, imag_part, precision=HIGHEST) + jnp.einsum(
        pattern, sine, real_part, precision=HIGHEST
    )
    return (out_real, out_imag)


def dft_table(length, sign):
    index_vals = jnp.arange(length, dtype=jnp.int32)
    exponent = index_vals[:, None] * index_vals[None, :] % length
    angle = sign * 2.0 * math.pi * exponent.astype(jnp.float32) / length
    return (jnp.cos(angle), jnp.sin(angle))


def channel_local(signal, filt):
    length, cols = signal.shape
    fft_length = 2 * length
    size_a = math.gcd(length, 1 << fft_length.bit_length() // 2)
    size_b = fft_length // size_a
    half_b = size_b // 2
    pair_cols = cols // 2
    paired = signal.reshape(half_b, size_a, pair_cols, 2)
    sig_real = paired[..., 0]
    sig_imag = paired[..., 1]
    filt_real = filt.reshape(half_b, size_a, pair_cols, 2)[..., 0]
    b_cos, b_sin = dft_table(size_b, -1.0)
    in_cos = b_cos[:, :half_b]
    in_sin = b_sin[:, :half_b]
    data_real, data_imag = table_apply("kb,bap->kap", in_cos, in_sin, sig_real, sig_imag)
    spec_real = jnp.einsum("kb,bap->kap", in_cos, filt_real, precision=HIGHEST)
    spec_imag = jnp.einsum("kb,bap->kap", in_sin, filt_real, precision=HIGHEST)
    fine_index = jnp.arange(size_b, dtype=jnp.int32)
    coarse_index = jnp.arange(size_a, dtype=jnp.int32)
    exponent = fine_index[:, None] * coarse_index[None, :] % fft_length
    tw_angle = -2.0 * math.pi * exponent.astype(jnp.float32) / fft_length
    tw_cos = jnp.cos(tw_angle)[:, :, None]
    tw_sin = jnp.sin(tw_angle)[:, :, None]
    data_real, data_imag = rotate(data_real, data_imag, tw_cos, tw_sin)
    spec_real, spec_imag = rotate(spec_real, spec_imag, tw_cos, tw_sin)
    a_cos, a_sin = dft_table(size_a, -1.0)
    data_real, data_imag = table_apply("ka,bap->bkp", a_cos, a_sin, data_real, data_imag)
    spec_real, spec_imag = table_apply("ka,bap->bkp", a_cos, a_sin, spec_real, spec_imag)
    prod_real = data_real * spec_real - data_imag * spec_imag
    prod_imag = data_real * spec_imag + data_imag * spec_real
    back_real, back_imag = table_apply("ak,bkp->bap", a_cos, -a_sin, prod_real, prod_imag)
    back_real, back_imag = rotate(back_real, back_imag, tw_cos, -tw_sin)
    final_real, final_imag = table_apply(
        "bk,kap->bap", b_cos[:half_b], -b_sin[:half_b], back_real, back_imag
    )
    joined = jnp.stack([final_real, final_imag], axis=-1).reshape(length, cols)
    return joined / fft_length


def plain(output_gate, input_gate, value_input, short_filter, long_filter, skip_gain):
    row_count, chan_count = value_input.shape
    group_total = long_filter.shape[1]
    tap_count = short_filter.shape[0]
    earlier = passed_along(value_input[row_count - tap_count + 1 :], "ctx", 1)
    extended = jnp.concatenate([earlier, value_input], axis=0).astype(jnp.float32)
    gated = input_gate.astype(jnp.float32) * depthwise(extended, short_filter)
    widened = jnp.repeat(long_filter, chan_count // group_total, axis=1)
    moved = (
        lax.all_to_all(gated, "ctx", split_axis=1, concat_axis=0, tiled=True),
        lax.all_to_all(widened, "ctx", split_axis=1, concat_axis=0, tiled=True),
    )
    convolved = channel_local(moved[0], moved[1])
    long_out = lax.all_to_all(convolved, "ctx", split_axis=0, concat_axis=1, tiled=True)
    mixed = output_gate.astype(jnp.float32) * (long_out + skip_gain[None, :] * gated)
    return mixed.astype(jnp.bfloat16)


def split(values):
    high = values.astype(jnp.bfloat16)
    return high, (values - high.astype(jnp.float32)).astype(jnp.bfloat16)


def split_table(table):
    high = table.astype(np.float32).astype(jnp.bfloat16)
    low = (table - high.astype(np.float64)).astype(np.float32).astype(jnp.bfloat16)
    return np.stack([high, low])


@functools.lru_cache
def tables(half):
    bins = np.arange(half)[:, None] + 0.5
    angle = 2.0 * np.pi * bins * np.arange(2 * half)[None, :] / (2 * half)
    forward = np.concatenate([np.cos(angle), -np.sin(angle)], 0)
    return forward, forward.T / half


def turning(rows, lanes):
    angle = 2.0 * np.pi * (np.arange(rows // 2) + 0.5) / (2 * rows)
    both = np.concatenate([np.cos(angle), -np.sin(angle)]).astype(np.float32)
    return np.repeat(both[:, None], lanes, 1)


def widening(groups, lanes):
    one = np.kron(np.eye(groups), np.ones((1, lanes // groups)))
    return np.kron(np.eye(2), one).astype(jnp.bfloat16)


def dot(a, b):
    return jnp.dot(a, b, preferred_element_type=jnp.float32)


def dot3(table, values):
    high, low = split(values)
    cols = values.shape[1]
    both = dot(table[0], jnp.concatenate([high, low], 1))
    return both[:, :cols] + both[:, cols:] + dot(table[1], high)


def scale_of(top):
    return jnp.maximum(top * 1.01, TINY).astype(jnp.bfloat16).astype(jnp.float32)


def to_code(values, scale):
    power = jnp.exp2(jnp.abs(values) * (SPAN / scale) - BIAS)
    return jnp.where(values < 0.0, -power, power).astype(jnp.bfloat16)


def from_code(code, scale):
    power = code.astype(jnp.float32)
    size = (jnp.log(jnp.abs(power)) * (1.0 / math.log(2.0)) + BIAS) * (scale * (1.0 / SPAN))
    return jnp.where(power < 0.0, -size, size)


def short_rows(ext, taps_spec, fwd, inv):
    count = taps_spec.shape[0] // 2
    rows, cols = ext.shape
    starts = range(0, rows - count, count)
    wide = jnp.concatenate([ext[s : s + 2 * count] for s in starts], 1)
    spec = dot(fwd[0], wide) + dot(fwd[1], wide)
    t_re = jnp.concatenate([taps_spec[:count]] * len(starts), 1)
    t_im = jnp.concatenate([taps_spec[count:]] * len(starts), 1)
    s_re, s_im = spec[:count], spec[count:]
    prod = jnp.concatenate([s_re * t_re - s_im * t_im, s_re * t_im + s_im * t_re], 0)
    back = dot3(inv, prod)
    return jnp.concatenate([back[:, w * cols : (w + 1) * cols] for w in range(len(starts))], 0)


IN_VMEM = pl.BlockSpec(memory_space=pltpu.VMEM)
IN_SMEM = pl.BlockSpec(memory_space=pltpu.SMEM)
IN_ANY = pl.BlockSpec(memory_space=pl.ANY)
IN_HBM = pl.BlockSpec(memory_space=pltpu.HBM)


def kernel_params(mib):
    return pltpu.CompilerParams(vmem_limit_bytes=mib * MIB)


def cost(scale):
    return pl.CostEstimate(flops=0, bytes_accessed=0, transcendentals=0)


def lanes_of(slab):
    return pl.ds(pl.multiple_of(slab * LANES, LANES), LANES)


def pace_body(me, out):
    out[0] = me[0]


def pace_call(me):
    return pl.pallas_call(
        pace_body,
        in_specs=[IN_SMEM],
        out_specs=IN_SMEM,
        out_shape=jax.ShapeDtypeStruct((1,), jnp.int32),
        compiler_params=kernel_params(4),
        cost_estimate=pl.CostEstimate(flops=10_000_000_000, bytes_accessed=8, transcendentals=0),
        name="pace",
    )(me)


def main_body(me, value, gate, taps, fwd, inv, gated, spec_out):
    count = taps.shape[0]
    wide = 2 * LANES
    for c in range(0, value.shape[1], wide):
        cols = slice(c, c + wide)
        taps_spec = dot3(fwd[:, :, :count], taps[:, cols])
        spec_out[:, cols] = taps_spec
        short = short_rows(value[:, cols], taps_spec, fwd, inv)
        gated[:, cols] = gate[count:, cols].astype(jnp.float32) * short


def main_call(me, value, gate, taps, fwd, inv, after):
    rows, chans = value.shape
    count = taps.shape[0]
    return pl.pallas_call(
        drop_after(main_body, 6, len(after)),
        in_specs=[IN_SMEM] + [IN_VMEM] * 5 + [IN_ANY] * len(after),
        out_specs=[IN_VMEM] * 2,
        out_shape=[
            jax.ShapeDtypeStruct((rows - count, chans), jnp.float32),
            jax.ShapeDtypeStruct((2 * count, chans), jnp.float32),
        ],
        compiler_params=kernel_params(12),
        cost_estimate=cost(4),
        name="short_main",
    )(me, value, gate, taps, fwd, inv, *after)


def drop_after(body, keep, unused):
    return lambda *refs: body(*refs[:keep], *refs[keep + unused :])


def write_code(code, values, filter_rows):
    groups = 8
    rows = sum(v.shape[0] for v in values)
    peak = functools.reduce(
        jnp.maximum, [jnp.max(jnp.abs(v), axis=0, keepdims=True) for v in values]
    )
    scale = scale_of(peak)
    start = 0
    for v in values:
        code[start : start + v.shape[0]] = to_code(v, scale)
        start += v.shape[0]
    scale = jnp.broadcast_to(scale, (groups, LANES))
    if filter_rows is None:
        both = scale
    else:
        size = jnp.abs(filter_rows)
        many = filter_rows.shape[0] // groups
        most = size[:groups]
        for c in range(1, many):
            most = jnp.maximum(most, size[c * groups : (c + 1) * groups])
        filter_scale = scale_of(jnp.max(most, axis=1, keepdims=True))
        filter_scale = jnp.broadcast_to(filter_scale, (groups, LANES))
        row, lane = (lax.broadcasted_iota(jnp.int32, scale.shape, k) for k in (0, 1))
        by_lane = jnp.sum(jnp.where(row == lane, filter_scale, 0.0), axis=0, keepdims=True)
        both = jnp.where(row == groups - 1, by_lane, scale)
        end = rows + filter_rows.shape[0]
        code[rows:end] = to_code(filter_rows, jnp.concatenate([filter_scale] * many, 0))
        rows = end
    code[rows:] = both.astype(jnp.bfloat16)


def ahead_body(part, me, value, gate, taps, long_taps, fwd, inv, *codes):
    count = taps.shape[0]
    for d, code in zip(part, codes):
        slab = me[0] ^ d
        cols = lanes_of(slab)
        taps_spec = dot3(fwd[:, :, :count], taps[:, cols])
        short = short_rows(value[:, cols], taps_spec, fwd, inv)
        write_code(code, [gate[count:, cols].astype(jnp.float32) * short], long_taps[slab])


def ahead_call(part, me, value, gate, taps, long_taps, fwd, inv, after):
    rows = value.shape[0] - taps.shape[0] + TILE + long_taps.shape[1]
    code = jax.ShapeDtypeStruct((rows, LANES), jnp.bfloat16)
    return pl.pallas_call(
        drop_after(functools.partial(ahead_body, part), 7, len(after)),
        in_specs=[IN_SMEM] + [IN_VMEM] * 6 + [IN_ANY] * len(after),
        out_specs=[IN_VMEM] * len(part),
        out_shape=[code] * len(part),
        compiler_params=kernel_params(12),
        cost_estimate=cost(1),
        name="short_ahead",
    )(me, value, gate, taps, long_taps, fwd, inv, *after)


def head_body(part, ahead, me, halo, value, gate, gated, taps_spec, long_taps, fwd, inv, *outs):
    taps = halo.shape[0]
    tops, codes = outs[: len(part)], outs[len(part) :]
    for d, top, code in zip(part, tops, codes):
        slab = me[0] ^ d
        cols = lanes_of(slab)
        ext = jnp.concatenate([halo[:, cols], value[:taps, cols]], 0)
        short = short_rows(ext, taps_spec[:, cols], fwd, inv)
        first = gate[:taps, cols].astype(jnp.float32) * short
        top[...] = first
        if d in ahead:
            write_code(code, [first], None)
        else:
            write_code(code, [first, gated[:, cols]], long_taps[slab])


def head_call(part, ahead, me, halo, value, gate, gated, taps_spec, long_taps, fwd, inv, after):
    taps = halo.shape[0]
    whole = taps + gated.shape[0] + TILE + long_taps.shape[1]
    codes = [
        jax.ShapeDtypeStruct((taps + TILE if d in ahead else whole, LANES), jnp.bfloat16)
        for d in part
    ]
    top = jax.ShapeDtypeStruct((taps, LANES), jnp.float32)
    return pl.pallas_call(
        drop_after(functools.partial(head_body, part, ahead), 9, len(after)),
        in_specs=[IN_SMEM] + [IN_VMEM] * 8 + [IN_ANY] * len(after),
        out_specs=[IN_VMEM] * (2 * len(part)),
        out_shape=[top] * len(part) + codes,
        compiler_params=kernel_params(12),
        cost_estimate=cost(len(part)),
        name="short_head",
    )(me, halo, value, gate, gated, taps_spec, long_taps, fwd, inv, *after)


def forward_body(d, clear, pieces, me, fwd, turn, widen, *rest):
    spec_out, filter_out, held_x, held_h = rest[-4:]
    rows = held_x.shape[0]
    half = rows // 2
    groups = 8
    end = rows
    for code, length in zip(rest, pieces):
        scales = code[code.shape[0] - TILE :].astype(jnp.float32)
        held_x[end - length : end] = from_code(code[:length], scales[:1])
        end -= length
    code, length = rest[0], pieces[0]
    scales = code[code.shape[0] - TILE :].astype(jnp.float32)
    row, lane = (lax.broadcasted_iota(jnp.int32, scales.shape, k) for k in (0, 1))
    by_lane = jnp.where(row == lane, scales[groups - 1 :], 0.0)
    scale = jnp.broadcast_to(jnp.sum(by_lane, axis=1, keepdims=True), scales.shape)
    taps = code[length : code.shape[0] - TILE]
    many = taps.shape[0] // groups
    h_high, h_low = split(from_code(taps, jnp.concatenate([scale] * many, 0)))
    h_high, h_low = h_high.astype(jnp.float32), h_low.astype(jnp.float32)
    for c in range(many):
        at = slice(c * groups, (c + 1) * groups)
        pair = jnp.concatenate([h_high[at], h_low[at]], 0).T.astype(jnp.bfloat16)
        wide = dot(pair, widen[...])
        for k in range(2):
            held_h[k, c * LANES : (c + 1) * LANES] = wide[:, k * LANES : (k + 1) * LANES]
    highs, lows = [], []
    for odd in range(2):
        step = pl.ds(odd, half, stride=2)
        high, low = split(held_x[step])
        highs += [high, held_h[0, step].astype(jnp.bfloat16)]
        lows += [low, held_h[1, step].astype(jnp.bfloat16)]
    width = 4 * LANES
    both = dot(fwd[0], jnp.concatenate(highs + lows, 1))
    both = both[:, :width] + both[:, width:] + dot(fwd[1], jnp.concatenate(highs, 1))
    w_re, w_im = turn[:half], turn[half:]
    outs = []
    for at in range(2):
        even = both[:, at * LANES : (at + 1) * LANES]
        odd = both[:, (2 + at) * LANES : (3 + at) * LANES]
        o_re, o_im = odd[:half], odd[half:]
        t_re = o_re * w_re - o_im * w_im
        t_im = o_re * w_im + o_im * w_re
        outs.append((even[:half] + t_re, even[:half] - t_re, even[half:] + t_im, even[half:] - t_im))
    for c, piece in enumerate(outs[0]):
        spec_out[c * half : (c + 1) * half] = piece
    if clear:
        filter_out[...] = jnp.zeros_like(filter_out)
    own = me[0] ^ d
    later = jnp.where(own + 1 < filter_out.shape[0] - 2, own + 1, own + 2)
    odd = lax.broadcasted_iota(jnp.int32, (half, LANES), 0) % 2 == 1
    for c, piece in enumerate(outs[1]):
        filter_out[own, c * half : (c + 1) * half] += piece
        moved = jnp.where(odd, -piece, piece) if c < 2 else jnp.where(odd, piece, -piece)
        at = slice(((c + 2) % 4) * half, ((c + 2) % 4 + 1) * half)
        filter_out[later, at] += moved


def forward_call(d, count, me, codes, fwd, turn, widen, early, so_far, after):
    rows = 2 * fwd.shape[2]
    held = so_far + early
    last = codes[-1].shape[0] - TILE
    pieces = [rows - last, last] if len(codes) > 1 else [rows]
    return pl.pallas_call(
        functools.partial(forward_body, d, not so_far, pieces),
        in_specs=[IN_SMEM] + [IN_VMEM] * (3 + len(codes) + len(held)) + [IN_ANY] * len(after),
        out_specs=[IN_VMEM] * 2,
        out_shape=[
            jax.ShapeDtypeStruct((2 * rows, LANES), jnp.float32),
            jax.ShapeDtypeStruct((count + 2, 2 * rows, LANES), jnp.float32),
        ],
        scratch_shapes=[
            pltpu.VMEM((rows, LANES), jnp.float32),
            pltpu.VMEM((2, rows, LANES), jnp.float32),
        ],
        input_output_aliases={4 + len(codes): 1} if so_far else {},
        compiler_params=kernel_params(12),
        cost_estimate=cost(1),
        name="forward",
    )(me, fwd, turn, widen, *codes, *held, *after)


def back_body(part, count, me_ref, filt, inv, turn, *refs):
    specs, codes, total, held = refs[:count], refs[-2 - len(part) : -2], refs[-2], refs[-1]
    rows = held.shape[0]
    half = rows // 2
    me = me_ref[0]

    for e, code in zip(part, codes):
        lags = []
        for d in range(count):
            lag = (me ^ e) - (me ^ d)
            lags.append(jnp.where(lag >= 0, lag, count))

        def chunk(c, _):
            def piece(start):
                return pl.ds(pl.multiple_of(start + c * 8, 8), 8)

            sums = []
            for start in (0, half):
                re, im = piece(start), piece(rows + start)
                acc_re = jnp.zeros((8, LANES), jnp.float32)
                acc_im = acc_re
                for d in range(count):
                    x_re, x_im = specs[d][re], specs[d][im]
                    g_re, g_im = filt[lags[d], re], filt[lags[d], im]
                    acc_re += x_re * g_re - x_im * g_im
                    acc_im += x_re * g_im + x_im * g_re
                sums += [acc_re, acc_im]
            a_re, a_im, b_re, b_im = sums
            re, im = piece(0), piece(half)
            w_re, w_im = turn[re], turn[im]
            d_re, d_im = a_re - b_re, a_im - b_im
            total[re, :LANES] = a_re + b_re
            total[im, :LANES] = a_im + b_im
            total[re, LANES:] = d_re * w_re + d_im * w_im
            total[im, LANES:] = d_im * w_re - d_re * w_im
            return 0

        lax.fori_loop(0, half // 8, chunk, 0, unroll=4)
        values = dot3(inv, total[...])
        held[pl.ds(0, half, stride=2)] = values[:, :LANES]
        held[pl.ds(1, half, stride=2)] = values[:, LANES:]
        peak = jnp.max(jnp.abs(values), axis=0, keepdims=True)
        scale = scale_of(jnp.maximum(peak[:, :LANES], peak[:, LANES:]))
        code[:rows] = to_code(held[...], scale)
        code[rows:] = jnp.broadcast_to(scale, (TILE, LANES)).astype(jnp.bfloat16)


def back_call(part, me, filt, inv, turn, specs, after):
    count = len(specs)
    bins = specs[0].shape[0]
    code = jax.ShapeDtypeStruct((bins // 2 + TILE, LANES), jnp.bfloat16)
    return pl.pallas_call(
        functools.partial(back_body, part, count),
        in_specs=[IN_SMEM] + [IN_VMEM] * (3 + count) + [IN_ANY] * len(after),
        out_specs=[IN_VMEM] * len(part),
        out_shape=[code] * len(part),
        scratch_shapes=[
            pltpu.VMEM((bins // 2, 2 * LANES), jnp.float32),
            pltpu.VMEM((bins // 2, LANES), jnp.float32),
        ],
        compiler_params=kernel_params(12),
        cost_estimate=cost(len(part)),
        name="back",
    )(me, filt, inv, turn, *specs, *after)


def final_body(part, count, me, *refs):
    many = len(part)
    codes, tops, (gated, gate, skip) = refs[:many], refs[many : 2 * many], refs[2 * many : 2 * many + 3]
    out, held, sems = refs[-3:]
    taps = tops[0].shape[0]
    rows = gate.shape[0]
    copies = []
    for at, d in enumerate(part):
        cols = lanes_of(me[0] ^ d)
        code, top = codes[at], tops[at]
        scale = code[rows : rows + 1].astype(jnp.float32)
        for r, part_gated in ((slice(0, taps), top[...]), (slice(taps, rows), gated[:, cols])):
            total = from_code(code[r], scale) + skip[:, cols] * part_gated
            held[at, r] = (gate[r, cols].astype(jnp.float32) * total).astype(jnp.bfloat16)
        copies.append(pltpu.make_async_copy(held.at[at], out.at[:, cols], sems.at[at]))
        copies[-1].start()
    for copy in copies:
        copy.wait()


def final_call(part, count, me, codes, tops, gated, gate, skip, so_far, after):
    rows = gate.shape[0]
    many = len(part)
    args = [me, *codes, *tops, gated, gate, skip]
    specs = [IN_SMEM] + [IN_VMEM] * (2 * many + 3)
    alias = {}
    if so_far:
        alias = {len(args): 0}
    args += so_far + after
    specs += [IN_HBM] * len(so_far) + [IN_ANY] * len(after)
    return pl.pallas_call(
        functools.partial(final_body, part, count),
        in_specs=specs,
        out_specs=IN_HBM,
        out_shape=jax.ShapeDtypeStruct(gate.shape, jnp.bfloat16),
        scratch_shapes=[
            pltpu.VMEM((many, rows, LANES), jnp.bfloat16),
            pltpu.SemaphoreType.DMA((many,)),
        ],
        input_output_aliases=alias,
        compiler_params=kernel_params(12),
        cost_estimate=cost(many),
        name="final",
    )(*args)


def in_slabs(output_gate, input_gate, value_input, short_filter, long_filter, skip_gain):
    count = lax.axis_size("ctx")
    me = lax.axis_index("ctx").reshape(1)
    rows = value_input.shape[0]
    taps = short_filter.shape[0]
    groups = long_filter.shape[1] // count

    def exchanged(block, d):
        return lax.ppermute(block, "ctx", [(i, i ^ d) for i in range(count)]) if d else block

    def table(values):
        return jnp.asarray(split_table(values))

    halo = passed_along(value_input[rows - taps :], "ctx", 1)
    long_taps = long_filter.T.reshape(count, groups, rows // LANES, LANES)
    long_taps = jnp.swapaxes(long_taps, 1, 2).reshape(count, -1, LANES)

    forward, inverse = tables(taps)
    short_fwd, short_inv = table(forward), table(inverse[taps:])
    half = rows // 2
    forward, inverse = tables(half)
    fwd, inv = table(forward[:, :half]), table(inverse[:half] / 2)
    turn = jnp.asarray(turning(rows, LANES))
    widen = jnp.asarray(widening(groups, LANES))

    came, tops, specs, answers = {}, {}, {}, {}
    after, filt, mixed = [], [], []

    paced = pace_call(me)
    main_out = []

    def mains():
        main_out[:] = main_call(
            paced, value_input, input_gate, short_filter, short_fwd, short_inv, after
        )
        after[:] = main_out[:1]

    def aheads(*part):
        codes = ahead_call(
            part, paced, value_input, input_gate, short_filter, long_taps, short_fwd, short_inv,
            after,
        )
        after[:] = codes[:1]
        for d, code in zip(part, codes):
            came[d] = [exchanged(code, d)]

    def heads(*part):
        outs = head_call(
            part, tuple(came), me, halo, value_input, input_gate, *main_out, long_taps,
            short_fwd, short_inv, after,
        )
        after[:] = outs[:1]
        for d, top, code in zip(part, outs, outs[len(part) :]):
            tops[d] = top
            came[d] = came.get(d, []) + [exchanged(code, d)]

    def forwards(*part):
        for d in part:
            specs[d], filt[:] = (lambda a, b: (a, [b]))(
                *forward_call(
                    d, count, me, came[d], fwd, turn, widen, [] if d else [inv], filt, after
                )
            )
            after[:] = [specs[d]]

    def backs(*part):
        held = [specs[d] for d in range(count)]
        for e in part:
            (code,) = back_call([e], me, filt[0], inv, turn, held, after)
            answers[e] = exchanged(code, e)
            after[:] = [code]

    def finals(*part):
        mixed[:] = [
            final_call(
                part, count, me, [answers[e] for e in part], [tops[e] for e in part],
                main_out[0], output_gate, skip_gain[None], mixed, after,
            )
        ]
        after[:] = mixed

    mains()
    heads(4)
    heads(2)
    heads(3)
    heads(5)
    heads(6, 0)
    forwards(0)
    forwards(4)
    heads(1)
    forwards(2)
    heads(7)
    forwards(3)
    forwards(5)
    forwards(6)
    forwards(1)
    forwards(7)
    backs(4)
    backs(5)
    backs(6)
    backs(7)
    backs(3)
    backs(0)
    finals(0, 4)
    backs(2)
    finals(5)
    backs(1)
    finals(6)
    finals(7, 3, 2, 1)
    return mixed[0]


def local(output_gate, input_gate, value_input, short_filter, long_filter, skip_gain):
    count = lax.axis_size("ctx")
    rows, chans = value_input.shape
    taps = short_filter.shape[0]
    groups = long_filter.shape[1]
    fits = chans == LANES * count and groups == 8 * count and taps == LANES
    fits = fits and rows % (2 * LANES) == 0 and rows > taps and count & (count - 1) == 0
    run = in_slabs if fits else plain
    return run(output_gate, input_gate, value_input, short_filter, long_filter, skip_gain)


def solution(mesh):
    placed = (
        P("ctx", "ch"),
        P("ctx", "ch"),
        P("ctx", "ch"),
        P(None, "ch"),
        P("ctx", "ch"),
        P("ch"),
    )
    return jax.shard_map(
        local, mesh=mesh, in_specs=placed, out_specs=P("ctx", "ch"), check_vma=False
    )
```

```python
import functools
import math

import jax
import jax.numpy as jnp
import numpy as np
from jax import lax
from jax.experimental import pallas as pl
from jax.experimental.pallas import tpu as pltpu
from jax.sharding import PartitionSpec as P

HIGHEST = lax.Precision.HIGHEST
LANES = 128
TILE = 8
SPAN = 250.0
BIAS = 125.0
TINY = 1e-30
MIB = 1 << 20


def passed_along(block, axis, distance):
    devices = range(lax.axis_size(axis))
    route = [(i - distance, i) for i in devices if i - distance in devices]
    return lax.ppermute(block, axis, route)


def depthwise(extended, filter_taps):
    kernel = filter_taps[::-1][:, None, :]
    result = lax.conv_general_dilated(
        extended[None],
        kernel,
        (1,),
        "VALID",
        dimension_numbers=("NWC", "WIO", "NWC"),
        feature_group_count=extended.shape[1],
        precision=HIGHEST,
    )
    return result[0]


def rotate(real_part, imag_part, cosine, sine):
    return (real_part * cosine - imag_part * sine, real_part * sine + imag_part * cosine)


def table_apply(pattern, cosine, sine, real_part, imag_part):
    out_real = jnp.einsum(pattern, cosine, real_part, precision=HIGHEST) - jnp.einsum(
        pattern, sine, imag_part, precision=HIGHEST
    )
    out_imag = jnp.einsum(pattern, cosine, imag_part, precision=HIGHEST) + jnp.einsum(
        pattern, sine, real_part, precision=HIGHEST
    )
    return (out_real, out_imag)


def dft_table(length, sign):
    index_vals = jnp.arange(length, dtype=jnp.int32)
    exponent = index_vals[:, None] * index_vals[None, :] % length
    angle = sign * 2.0 * math.pi * exponent.astype(jnp.float32) / length
    return (jnp.cos(angle), jnp.sin(angle))


def channel_local(signal, filt):
    length, cols = signal.shape
    fft_length = 2 * length
    size_a = math.gcd(length, 1 << fft_length.bit_length() // 2)
    size_b = fft_length // size_a
    half_b = size_b // 2
    pair_cols = cols // 2
    paired = signal.reshape(half_b, size_a, pair_cols, 2)
    sig_real = paired[..., 0]
    sig_imag = paired[..., 1]
    filt_real = filt.reshape(half_b, size_a, pair_cols, 2)[..., 0]
    b_cos, b_sin = dft_table(size_b, -1.0)
    in_cos = b_cos[:, :half_b]
    in_sin = b_sin[:, :half_b]
    data_real, data_imag = table_apply("kb,bap->kap", in_cos, in_sin, sig_real, sig_imag)
    spec_real = jnp.einsum("kb,bap->kap", in_cos, filt_real, precision=HIGHEST)
    spec_imag = jnp.einsum("kb,bap->kap", in_sin, filt_real, precision=HIGHEST)
    fine_index = jnp.arange(size_b, dtype=jnp.int32)
    coarse_index = jnp.arange(size_a, dtype=jnp.int32)
    exponent = fine_index[:, None] * coarse_index[None, :] % fft_length
    tw_angle = -2.0 * math.pi * exponent.astype(jnp.float32) / fft_length
    tw_cos = jnp.cos(tw_angle)[:, :, None]
    tw_sin = jnp.sin(tw_angle)[:, :, None]
    data_real, data_imag = rotate(data_real, data_imag, tw_cos, tw_sin)
    spec_real, spec_imag = rotate(spec_real, spec_imag, tw_cos, tw_sin)
    a_cos, a_sin = dft_table(size_a, -1.0)
    data_real, data_imag = table_apply("ka,bap->bkp", a_cos, a_sin, data_real, data_imag)
    spec_real, spec_imag = table_apply("ka,bap->bkp", a_cos, a_sin, spec_real, spec_imag)
    prod_real = data_real * spec_real - data_imag * spec_imag
    prod_imag = data_real * spec_imag + data_imag * spec_real
    back_real, back_imag = table_apply("ak,bkp->bap", a_cos, -a_sin, prod_real, prod_imag)
    back_real, back_imag = rotate(back_real, back_imag, tw_cos, -tw_sin)
    final_real, final_imag = table_apply(
        "bk,kap->bap", b_cos[:half_b], -b_sin[:half_b], back_real, back_imag
    )
    joined = jnp.stack([final_real, final_imag], axis=-1).reshape(length, cols)
    return joined / fft_length


def plain(output_gate, input_gate, value_input, short_filter, long_filter, skip_gain):
    row_count, chan_count = value_input.shape
    group_total = long_filter.shape[1]
    tap_count = short_filter.shape[0]
    earlier = passed_along(value_input[row_count - tap_count + 1 :], "ctx", 1)
    extended = jnp.concatenate([earlier, value_input], axis=0).astype(jnp.float32)
    gated = input_gate.astype(jnp.float32) * depthwise(extended, short_filter)
    widened = jnp.repeat(long_filter, chan_count // group_total, axis=1)
    moved = (
        lax.all_to_all(gated, "ctx", split_axis=1, concat_axis=0, tiled=True),
        lax.all_to_all(widened, "ctx", split_axis=1, concat_axis=0, tiled=True),
    )
    convolved = channel_local(moved[0], moved[1])
    long_out = lax.all_to_all(convolved, "ctx", split_axis=0, concat_axis=1, tiled=True)
    mixed = output_gate.astype(jnp.float32) * (long_out + skip_gain[None, :] * gated)
    return mixed.astype(jnp.bfloat16)


def split(values):
    high = values.astype(jnp.bfloat16)
    return high, (values - high.astype(jnp.float32)).astype(jnp.bfloat16)


def split_table(table):
    high = table.astype(np.float32).astype(jnp.bfloat16)
    low = (table - high.astype(np.float64)).astype(np.float32).astype(jnp.bfloat16)
    return np.stack([high, low])


@functools.lru_cache
def tables(half):
    bins = np.arange(half)[:, None] + 0.5
    angle = 2.0 * np.pi * bins * np.arange(2 * half)[None, :] / (2 * half)
    forward = np.concatenate([np.cos(angle), -np.sin(angle)], 0)
    return forward, forward.T / half


def turning(rows, lanes):
    angle = 2.0 * np.pi * (np.arange(rows // 2) + 0.5) / (2 * rows)
    both = np.concatenate([np.cos(angle), -np.sin(angle)]).astype(np.float32)
    return np.repeat(both[:, None], lanes, 1)


def widening(groups, lanes):
    one = np.kron(np.eye(groups), np.ones((1, lanes // groups)))
    return np.kron(np.eye(2), one).astype(jnp.bfloat16)


def dot(a, b):
    return jnp.dot(a, b, preferred_element_type=jnp.float32)


def dot3(table, values):
    high, low = split(values)
    cols = values.shape[1]
    both = dot(table[0], jnp.concatenate([high, low], 1))
    return both[:, :cols] + both[:, cols:] + dot(table[1], high)


def scale_of(top):
    return jnp.maximum(top * 1.01, TINY).astype(jnp.bfloat16).astype(jnp.float32)


def to_code(values, scale):
    power = jnp.exp2(jnp.abs(values) * (SPAN / scale) - BIAS)
    return jnp.where(values < 0.0, -power, power).astype(jnp.bfloat16)


def from_code(code, scale):
    power = code.astype(jnp.float32)
    size = (jnp.log(jnp.abs(power)) * (1.0 / math.log(2.0)) + BIAS) * (scale * (1.0 / SPAN))
    return jnp.where(power < 0.0, -size, size)


def short_rows(ext, taps_spec, fwd, inv):
    count = taps_spec.shape[0] // 2
    rows, cols = ext.shape
    starts = range(0, rows - count, count)
    wide = jnp.concatenate([ext[s : s + 2 * count] for s in starts], 1)
    spec = dot(fwd[0], wide) + dot(fwd[1], wide)
    t_re = jnp.concatenate([taps_spec[:count]] * len(starts), 1)
    t_im = jnp.concatenate([taps_spec[count:]] * len(starts), 1)
    s_re, s_im = spec[:count], spec[count:]
    prod = jnp.concatenate([s_re * t_re - s_im * t_im, s_re * t_im + s_im * t_re], 0)
    back = dot3(inv, prod)
    return jnp.concatenate([back[:, w * cols : (w + 1) * cols] for w in range(len(starts))], 0)


IN_VMEM = pl.BlockSpec(memory_space=pltpu.VMEM)
IN_SMEM = pl.BlockSpec(memory_space=pltpu.SMEM)
IN_ANY = pl.BlockSpec(memory_space=pl.ANY)
IN_HBM = pl.BlockSpec(memory_space=pltpu.HBM)


def kernel_params(mib):
    return pltpu.CompilerParams(vmem_limit_bytes=mib * MIB)


def cost(scale):
    return pl.CostEstimate(flops=0, bytes_accessed=0, transcendentals=0)


def lanes_of(slab):
    return pl.ds(pl.multiple_of(slab * LANES, LANES), LANES)


def pace_body(me, out):
    out[0] = me[0]


def pace_call(me):
    return pl.pallas_call(
        pace_body,
        in_specs=[IN_SMEM],
        out_specs=IN_SMEM,
        out_shape=jax.ShapeDtypeStruct((1,), jnp.int32),
        compiler_params=kernel_params(4),
        cost_estimate=pl.CostEstimate(flops=10_000_000_000, bytes_accessed=8, transcendentals=0),
        name="pace",
    )(me)


def main_body(me, value, gate, taps, fwd, inv, gated, spec_out):
    count = taps.shape[0]
    wide = 2 * LANES
    for c in range(0, value.shape[1], wide):
        cols = slice(c, c + wide)
        taps_spec = dot3(fwd[:, :, :count], taps[:, cols])
        spec_out[:, cols] = taps_spec
        short = short_rows(value[:, cols], taps_spec, fwd, inv)
        gated[:, cols] = gate[count:, cols].astype(jnp.float32) * short


def main_call(me, value, gate, taps, fwd, inv, after):
    rows, chans = value.shape
    count = taps.shape[0]
    return pl.pallas_call(
        drop_after(main_body, 6, len(after)),
        in_specs=[IN_SMEM] + [IN_VMEM] * 5 + [IN_ANY] * len(after),
        out_specs=[IN_VMEM] * 2,
        out_shape=[
            jax.ShapeDtypeStruct((rows - count, chans), jnp.float32),
            jax.ShapeDtypeStruct((2 * count, chans), jnp.float32),
        ],
        compiler_params=kernel_params(12),
        cost_estimate=cost(4),
        name="short_main",
    )(me, value, gate, taps, fwd, inv, *after)


def drop_after(body, keep, unused):
    return lambda *refs: body(*refs[:keep], *refs[keep + unused :])


def write_code(code, values, filter_rows):
    groups = 8
    rows = sum(v.shape[0] for v in values)
    peak = functools.reduce(
        jnp.maximum, [jnp.max(jnp.abs(v), axis=0, keepdims=True) for v in values]
    )
    scale = scale_of(peak)
    start = 0
    for v in values:
        code[start : start + v.shape[0]] = to_code(v, scale)
        start += v.shape[0]
    scale = jnp.broadcast_to(scale, (groups, LANES))
    size = jnp.abs(filter_rows)
    many = filter_rows.shape[0] // groups
    most = size[:groups]
    for c in range(1, many):
        most = jnp.maximum(most, size[c * groups : (c + 1) * groups])
    filter_scale = scale_of(jnp.max(most, axis=1, keepdims=True))
    filter_scale = jnp.broadcast_to(filter_scale, (groups, LANES))
    row, lane = (lax.broadcasted_iota(jnp.int32, scale.shape, k) for k in (0, 1))
    by_lane = jnp.sum(jnp.where(row == lane, filter_scale, 0.0), axis=0, keepdims=True)
    both = jnp.where(row == groups - 1, by_lane, scale)
    end = rows + filter_rows.shape[0]
    code[rows:end] = to_code(filter_rows, jnp.concatenate([filter_scale] * many, 0))
    rows = end
    code[rows:] = both.astype(jnp.bfloat16)


def head_body(part, me, halo, value, gate, gated, taps_spec, long_taps, fwd, inv, *outs):
    taps = halo.shape[0]
    tops, codes = outs[: len(part)], outs[len(part) :]
    for d, top, code in zip(part, tops, codes):
        slab = me[0] ^ d
        cols = lanes_of(slab)
        ext = jnp.concatenate([halo[:, cols], value[:taps, cols]], 0)
        short = short_rows(ext, taps_spec[:, cols], fwd, inv)
        first = gate[:taps, cols].astype(jnp.float32) * short
        top[...] = first
        write_code(code, [first, gated[:, cols]], long_taps[slab])


def head_call(part, me, halo, value, gate, gated, taps_spec, long_taps, fwd, inv, after):
    taps = halo.shape[0]
    whole = taps + gated.shape[0] + TILE + long_taps.shape[1]
    codes = [jax.ShapeDtypeStruct((whole, LANES), jnp.bfloat16)] * len(part)
    top = jax.ShapeDtypeStruct((taps, LANES), jnp.float32)
    return pl.pallas_call(
        drop_after(functools.partial(head_body, part), 9, len(after)),
        in_specs=[IN_SMEM] + [IN_VMEM] * 8 + [IN_ANY] * len(after),
        out_specs=[IN_VMEM] * (2 * len(part)),
        out_shape=[top] * len(part) + codes,
        compiler_params=kernel_params(12),
        cost_estimate=cost(len(part)),
        name="short_head",
    )(me, halo, value, gate, gated, taps_spec, long_taps, fwd, inv, *after)


def forward_body(d, clear, me, code, fwd, turn, widen, *rest):
    spec_out, filter_out, held_x, held_h = rest[-4:]
    rows = held_x.shape[0]
    half = rows // 2
    groups = 8
    scales = code[code.shape[0] - TILE :].astype(jnp.float32)
    held_x[...] = from_code(code[:rows], scales[:1])
    row, lane = (lax.broadcasted_iota(jnp.int32, scales.shape, k) for k in (0, 1))
    by_lane = jnp.where(row == lane, scales[groups - 1 :], 0.0)
    scale = jnp.broadcast_to(jnp.sum(by_lane, axis=1, keepdims=True), scales.shape)
    taps = code[rows : code.shape[0] - TILE]
    many = taps.shape[0] // groups
    h_high, h_low = split(from_code(taps, jnp.concatenate([scale] * many, 0)))
    h_high, h_low = h_high.astype(jnp.float32), h_low.astype(jnp.float32)
    for c in range(many):
        at = slice(c * groups, (c + 1) * groups)
        pair = jnp.concatenate([h_high[at], h_low[at]], 0).T.astype(jnp.bfloat16)
        wide = dot(pair, widen[...])
        for k in range(2):
            held_h[k, c * LANES : (c + 1) * LANES] = wide[:, k * LANES : (k + 1) * LANES]
    highs, lows = [], []
    for odd in range(2):
        step = pl.ds(odd, half, stride=2)
        high, low = split(held_x[step])
        highs += [high, held_h[0, step].astype(jnp.bfloat16)]
        lows += [low, held_h[1, step].astype(jnp.bfloat16)]
    width = 4 * LANES
    both = dot(fwd[0], jnp.concatenate(highs + lows, 1))
    both = both[:, :width] + both[:, width:] + dot(fwd[1], jnp.concatenate(highs, 1))
    w_re, w_im = turn[:half], turn[half:]
    outs = []
    for at in range(2):
        even = both[:, at * LANES : (at + 1) * LANES]
        odd = both[:, (2 + at) * LANES : (3 + at) * LANES]
        o_re, o_im = odd[:half], odd[half:]
        t_re = o_re * w_re - o_im * w_im
        t_im = o_re * w_im + o_im * w_re
        outs.append((even[:half] + t_re, even[:half] - t_re, even[half:] + t_im, even[half:] - t_im))
    for c, piece in enumerate(outs[0]):
        spec_out[c * half : (c + 1) * half] = piece
    if clear:
        filter_out[...] = jnp.zeros_like(filter_out)
    own = me[0] ^ d
    later = jnp.where(own + 1 < filter_out.shape[0] - 2, own + 1, own + 2)
    odd = lax.broadcasted_iota(jnp.int32, (half, LANES), 0) % 2 == 1
    for c, piece in enumerate(outs[1]):
        filter_out[own, c * half : (c + 1) * half] += piece
        moved = jnp.where(odd, -piece, piece) if c < 2 else jnp.where(odd, piece, -piece)
        at = slice(((c + 2) % 4) * half, ((c + 2) % 4 + 1) * half)
        filter_out[later, at] += moved


def forward_call(d, count, me, code, fwd, turn, widen, early, so_far, after):
    rows = 2 * fwd.shape[2]
    held = so_far + early
    return pl.pallas_call(
        functools.partial(forward_body, d, not so_far),
        in_specs=[IN_SMEM] + [IN_VMEM] * (4 + len(held)) + [IN_ANY] * len(after),
        out_specs=[IN_VMEM] * 2,
        out_shape=[
            jax.ShapeDtypeStruct((2 * rows, LANES), jnp.float32),
            jax.ShapeDtypeStruct((count + 2, 2 * rows, LANES), jnp.float32),
        ],
        scratch_shapes=[
            pltpu.VMEM((rows, LANES), jnp.float32),
            pltpu.VMEM((2, rows, LANES), jnp.float32),
        ],
        input_output_aliases={5: 1} if so_far else {},
        compiler_params=kernel_params(12),
        cost_estimate=cost(1),
        name="forward",
    )(me, code, fwd, turn, widen, *held, *after)


def back_body(part, count, me_ref, filt, inv, turn, *refs):
    specs, codes, total, held = refs[:count], refs[-2 - len(part) : -2], refs[-2], refs[-1]
    rows = held.shape[0]
    half = rows // 2
    me = me_ref[0]

    for e, code in zip(part, codes):
        lags = []
        for d in range(count):
            lag = (me ^ e) - (me ^ d)
            lags.append(jnp.where(lag >= 0, lag, count))

        def chunk(c, _):
            def piece(start):
                return pl.ds(pl.multiple_of(start + c * 8, 8), 8)

            sums = []
            for start in (0, half):
                re, im = piece(start), piece(rows + start)
                acc_re = jnp.zeros((8, LANES), jnp.float32)
                acc_im = acc_re
                for d in range(count):
                    x_re, x_im = specs[d][re], specs[d][im]
                    g_re, g_im = filt[lags[d], re], filt[lags[d], im]
                    acc_re += x_re * g_re - x_im * g_im
                    acc_im += x_re * g_im + x_im * g_re
                sums += [acc_re, acc_im]
            a_re, a_im, b_re, b_im = sums
            re, im = piece(0), piece(half)
            w_re, w_im = turn[re], turn[im]
            d_re, d_im = a_re - b_re, a_im - b_im
            total[re, :LANES] = a_re + b_re
            total[im, :LANES] = a_im + b_im
            total[re, LANES:] = d_re * w_re + d_im * w_im
            total[im, LANES:] = d_im * w_re - d_re * w_im
            return 0

        lax.fori_loop(0, half // 8, chunk, 0, unroll=4)
        values = dot3(inv, total[...])
        held[pl.ds(0, half, stride=2)] = values[:, :LANES]
        held[pl.ds(1, half, stride=2)] = values[:, LANES:]
        peak = jnp.max(jnp.abs(values), axis=0, keepdims=True)
        scale = scale_of(jnp.maximum(peak[:, :LANES], peak[:, LANES:]))
        code[:rows] = to_code(held[...], scale)
        code[rows:] = jnp.broadcast_to(scale, (TILE, LANES)).astype(jnp.bfloat16)


def back_call(part, me, filt, inv, turn, specs, after):
    count = len(specs)
    bins = specs[0].shape[0]
    code = jax.ShapeDtypeStruct((bins // 2 + TILE, LANES), jnp.bfloat16)
    return pl.pallas_call(
        functools.partial(back_body, part, count),
        in_specs=[IN_SMEM] + [IN_VMEM] * (3 + count) + [IN_ANY] * len(after),
        out_specs=[IN_VMEM] * len(part),
        out_shape=[code] * len(part),
        scratch_shapes=[
            pltpu.VMEM((bins // 2, 2 * LANES), jnp.float32),
            pltpu.VMEM((bins // 2, LANES), jnp.float32),
        ],
        compiler_params=kernel_params(12),
        cost_estimate=cost(len(part)),
        name="back",
    )(me, filt, inv, turn, *specs, *after)


def finish(code, top, gated, gate, skip, cols, out):
    taps = top.shape[0]
    rows = gate.shape[0]
    scale = code[rows : rows + 1].astype(jnp.float32)
    for r, part_gated in ((slice(0, taps), top[...]), (slice(taps, rows), gated[:, cols])):
        total = from_code(code[r], scale) + skip[:, cols] * part_gated
        out[r] = (gate[r, cols].astype(jnp.float32) * total).astype(jnp.bfloat16)


def final_body(part, me, gated, gate, skip, *refs):
    many = len(part)
    codes, tops, outs = refs[:many], refs[many : 2 * many], refs[2 * many :]
    for d, code, top, out in zip(part, codes, tops, outs):
        finish(code, top, gated, gate, skip, lanes_of(me[0] ^ d), out)


def final_call(part, me, codes, tops, gated, gate, skip, after):
    many = len(part)
    slab = jax.ShapeDtypeStruct((gate.shape[0], LANES), jnp.bfloat16)
    return pl.pallas_call(
        drop_after(functools.partial(final_body, part), 4 + 2 * many, len(after)),
        in_specs=[IN_SMEM] + [IN_VMEM] * (3 + 2 * many) + [IN_ANY] * len(after),
        out_specs=[IN_VMEM] * many,
        out_shape=[slab] * many,
        compiler_params=kernel_params(12),
        cost_estimate=cost(many),
        name="final",
    )(me, gated, gate, skip, *codes, *tops, *after)


def last_body(part, ready, me, gated, gate, skip, *refs):
    many = len(part)
    codes, tops = refs[:many], refs[many : 2 * many]
    slabs, (out, held, sems) = refs[2 * many : -3], refs[-3:]
    copies = []

    def send(d, slab):
        at = len(copies)
        copies.append(pltpu.make_async_copy(slab, out.at[:, lanes_of(me[0] ^ d)], sems.at[at]))
        copies[-1].start()

    for d, slab in zip(ready, slabs):
        send(d, slab)
    for at, d in enumerate(part):
        finish(codes[at], tops[at], gated, gate, skip, lanes_of(me[0] ^ d), held.at[at])
        send(d, held.at[at])
    for copy in copies:
        copy.wait()


def last_call(part, me, codes, tops, gated, gate, skip, slabs):
    many = len(part)
    ready = tuple(slabs)
    return pl.pallas_call(
        functools.partial(last_body, part, ready),
        in_specs=[IN_SMEM] + [IN_VMEM] * (3 + 2 * many + len(ready)),
        out_specs=IN_ANY,
        out_shape=jax.ShapeDtypeStruct(gate.shape, jnp.bfloat16),
        scratch_shapes=[
            pltpu.VMEM((many, gate.shape[0], LANES), jnp.bfloat16),
            pltpu.SemaphoreType.DMA((many + len(ready),)),
        ],
        compiler_params=kernel_params(12),
        cost_estimate=cost(many),
        name="last",
    )(me, gated, gate, skip, *codes, *tops, *slabs.values())


def in_slabs(output_gate, input_gate, value_input, short_filter, long_filter, skip_gain):
    count = lax.axis_size("ctx")
    me = lax.axis_index("ctx").reshape(1)
    rows = value_input.shape[0]
    taps = short_filter.shape[0]
    groups = long_filter.shape[1] // count

    def exchanged(block, d):
        return lax.ppermute(block, "ctx", [(i, i ^ d) for i in range(count)]) if d else block

    def table(values):
        return jnp.asarray(split_table(values))

    paced = pace_call(me)
    start = rows - taps + jnp.minimum(paced[0], 0)
    halo = passed_along(lax.dynamic_slice_in_dim(value_input, start, taps, 0), "ctx", 1)
    long_taps = long_filter.T.reshape(count, groups, rows // LANES, LANES)
    long_taps = jnp.swapaxes(long_taps, 1, 2).reshape(count, -1, LANES)

    forward, inverse = tables(taps)
    short_fwd, short_inv = table(forward), table(inverse[taps:])
    half = rows // 2
    forward, inverse = tables(half)
    fwd, inv = table(forward[:, :half]), table(inverse[:half] / 2)
    turn = jnp.asarray(turning(rows, LANES))
    widen = jnp.asarray(widening(groups, LANES))

    came, tops, specs, answers = {}, {}, {}, {}
    after, filt, mixed = [], [], {}

    main_out = []

    def mains():
        main_out[:] = main_call(
            paced, value_input, input_gate, short_filter, short_fwd, short_inv, after
        )
        after[:] = main_out[:1]

    def heads(*part):
        outs = head_call(
            part, me, halo, value_input, input_gate, *main_out, long_taps,
            short_fwd, short_inv, after,
        )
        after[:] = outs[:1]
        for d, top, code in zip(part, outs, outs[len(part) :]):
            tops[d] = top
            came[d] = exchanged(code, d)

    def forwards(*part):
        for d in part:
            specs[d], filt[:] = (lambda a, b: (a, [b]))(
                *forward_call(
                    d, count, me, came[d], fwd, turn, widen, [] if d else [inv], filt, after
                )
            )
            after[:] = [specs[d]]

    def backs(*part):
        held = [specs[d] for d in range(count)]
        for e in part:
            (code,) = back_call([e], me, filt[0], inv, turn, held, after)
            answers[e] = exchanged(code, e)
            after[:] = [code]

    def finals(*part):
        args = [me, [answers[e] for e in part], [tops[e] for e in part]]
        args += [main_out[0], output_gate, skip_gain[None]]
        if len(mixed) + len(part) == count:
            return last_call(part, *args, mixed)
        outs = final_call(part, *args, after)
        mixed.update(zip(part, outs))
        after[:] = outs[:1]

    mains()
    heads(4)
    heads(2)
    heads(5)
    heads(3)
    heads(6, 0)
    forwards(0)
    forwards(4)
    heads(1)
    forwards(2)
    heads(7)
    forwards(5)
    forwards(3)
    forwards(6)
    forwards(1)
    forwards(7)
    backs(4)
    backs(5)
    backs(6)
    backs(7)
    backs(3)
    backs(0)
    finals(0, 4)
    backs(2)
    finals(5)
    backs(1)
    finals(6, 7)
    return finals(3, 2, 1)


def local(output_gate, input_gate, value_input, short_filter, long_filter, skip_gain):
    count = lax.axis_size("ctx")
    rows, chans = value_input.shape
    taps = short_filter.shape[0]
    groups = long_filter.shape[1]
    fits = chans == LANES * count and groups == 8 * count and taps == LANES
    fits = fits and rows % (2 * LANES) == 0 and rows > taps and count & (count - 1) == 0
    run = in_slabs if fits else plain
    return run(output_gate, input_gate, value_input, short_filter, long_filter, skip_gain)


def solution(mesh):
    placed = (
        P("ctx", "ch"),
        P("ctx", "ch"),
        P("ctx", "ch"),
        P(None, "ch"),
        P("ctx", "ch"),
        P("ch"),
    )
    return jax.shard_map(
        local, mesh=mesh, in_specs=placed, out_specs=P("ctx", "ch"), check_vma=False
    )
```

```python
import functools
import math

import jax
import jax.numpy as jnp
import numpy as np
from jax import lax
from jax.experimental import pallas as pl
from jax.experimental.pallas import tpu as pltpu
from jax.sharding import PartitionSpec as P

HIGHEST = lax.Precision.HIGHEST
LANES = 128
TILE = 8
SPAN = 250.0
BIAS = 125.0
TINY = 1e-30
MIB = 1 << 20


def passed_along(block, axis, distance):
    devices = range(lax.axis_size(axis))
    route = [(i - distance, i) for i in devices if i - distance in devices]
    return lax.ppermute(block, axis, route)


def depthwise(extended, filter_taps):
    kernel = filter_taps[::-1][:, None, :]
    result = lax.conv_general_dilated(
        extended[None],
        kernel,
        (1,),
        "VALID",
        dimension_numbers=("NWC", "WIO", "NWC"),
        feature_group_count=extended.shape[1],
        precision=HIGHEST,
    )
    return result[0]


def rotate(real_part, imag_part, cosine, sine):
    return (real_part * cosine - imag_part * sine, real_part * sine + imag_part * cosine)


def table_apply(pattern, cosine, sine, real_part, imag_part):
    out_real = jnp.einsum(pattern, cosine, real_part, precision=HIGHEST) - jnp.einsum(
        pattern, sine, imag_part, precision=HIGHEST
    )
    out_imag = jnp.einsum(pattern, cosine, imag_part, precision=HIGHEST) + jnp.einsum(
        pattern, sine, real_part, precision=HIGHEST
    )
    return (out_real, out_imag)


def dft_table(length, sign):
    index_vals = jnp.arange(length, dtype=jnp.int32)
    exponent = index_vals[:, None] * index_vals[None, :] % length
    angle = sign * 2.0 * math.pi * exponent.astype(jnp.float32) / length
    return (jnp.cos(angle), jnp.sin(angle))


def channel_local(signal, filt):
    length, cols = signal.shape
    fft_length = 2 * length
    size_a = math.gcd(length, 1 << fft_length.bit_length() // 2)
    size_b = fft_length // size_a
    half_b = size_b // 2
    pair_cols = cols // 2
    paired = signal.reshape(half_b, size_a, pair_cols, 2)
    sig_real = paired[..., 0]
    sig_imag = paired[..., 1]
    filt_real = filt.reshape(half_b, size_a, pair_cols, 2)[..., 0]
    b_cos, b_sin = dft_table(size_b, -1.0)
    in_cos = b_cos[:, :half_b]
    in_sin = b_sin[:, :half_b]
    data_real, data_imag = table_apply("kb,bap->kap", in_cos, in_sin, sig_real, sig_imag)
    spec_real = jnp.einsum("kb,bap->kap", in_cos, filt_real, precision=HIGHEST)
    spec_imag = jnp.einsum("kb,bap->kap", in_sin, filt_real, precision=HIGHEST)
    fine_index = jnp.arange(size_b, dtype=jnp.int32)
    coarse_index = jnp.arange(size_a, dtype=jnp.int32)
    exponent = fine_index[:, None] * coarse_index[None, :] % fft_length
    tw_angle = -2.0 * math.pi * exponent.astype(jnp.float32) / fft_length
    tw_cos = jnp.cos(tw_angle)[:, :, None]
    tw_sin = jnp.sin(tw_angle)[:, :, None]
    data_real, data_imag = rotate(data_real, data_imag, tw_cos, tw_sin)
    spec_real, spec_imag = rotate(spec_real, spec_imag, tw_cos, tw_sin)
    a_cos, a_sin = dft_table(size_a, -1.0)
    data_real, data_imag = table_apply("ka,bap->bkp", a_cos, a_sin, data_real, data_imag)
    spec_real, spec_imag = table_apply("ka,bap->bkp", a_cos, a_sin, spec_real, spec_imag)
    prod_real = data_real * spec_real - data_imag * spec_imag
    prod_imag = data_real * spec_imag + data_imag * spec_real
    back_real, back_imag = table_apply("ak,bkp->bap", a_cos, -a_sin, prod_real, prod_imag)
    back_real, back_imag = rotate(back_real, back_imag, tw_cos, -tw_sin)
    final_real, final_imag = table_apply(
        "bk,kap->bap", b_cos[:half_b], -b_sin[:half_b], back_real, back_imag
    )
    joined = jnp.stack([final_real, final_imag], axis=-1).reshape(length, cols)
    return joined / fft_length


def plain(output_gate, input_gate, value_input, short_filter, long_filter, skip_gain):
    row_count, chan_count = value_input.shape
    group_total = long_filter.shape[1]
    tap_count = short_filter.shape[0]
    earlier = passed_along(value_input[row_count - tap_count + 1 :], "ctx", 1)
    extended = jnp.concatenate([earlier, value_input], axis=0).astype(jnp.float32)
    gated = input_gate.astype(jnp.float32) * depthwise(extended, short_filter)
    widened = jnp.repeat(long_filter, chan_count // group_total, axis=1)
    moved = (
        lax.all_to_all(gated, "ctx", split_axis=1, concat_axis=0, tiled=True),
        lax.all_to_all(widened, "ctx", split_axis=1, concat_axis=0, tiled=True),
    )
    convolved = channel_local(moved[0], moved[1])
    long_out = lax.all_to_all(convolved, "ctx", split_axis=0, concat_axis=1, tiled=True)
    mixed = output_gate.astype(jnp.float32) * (long_out + skip_gain[None, :] * gated)
    return mixed.astype(jnp.bfloat16)


def split(values):
    high = values.astype(jnp.bfloat16)
    return high, (values - high.astype(jnp.float32)).astype(jnp.bfloat16)


def split_table(table):
    high = table.astype(np.float32).astype(jnp.bfloat16)
    low = (table - high.astype(np.float64)).astype(np.float32).astype(jnp.bfloat16)
    return np.stack([high, low])


@functools.lru_cache
def tables(half):
    bins = np.arange(half)[:, None] + 0.5
    angle = 2.0 * np.pi * bins * np.arange(2 * half)[None, :] / (2 * half)
    forward = np.concatenate([np.cos(angle), -np.sin(angle)], 0)
    return forward, forward.T / half


def turning(rows, lanes):
    angle = 2.0 * np.pi * (np.arange(rows // 2) + 0.5) / (2 * rows)
    both = np.concatenate([np.cos(angle), -np.sin(angle)]).astype(np.float32)
    return np.repeat(both[:, None], lanes, 1)


def widening(groups, lanes, pieces):
    one = np.kron(np.eye(groups), np.ones((1, lanes // groups)))
    return np.kron(np.eye(pieces), one).astype(jnp.bfloat16)


def dot(a, b):
    return jnp.dot(a, b, preferred_element_type=jnp.float32)


def dot3(table, values):
    high, low = split(values)
    cols = values.shape[1]
    both = dot(table[0], jnp.concatenate([high, low], 1))
    return both[:, :cols] + both[:, cols:] + dot(table[1], high)


def scale_of(top):
    return jnp.maximum(top * 1.01, TINY).astype(jnp.bfloat16).astype(jnp.float32)


def to_code(values, scale):
    power = jnp.exp2(jnp.abs(values) * (SPAN / scale) - BIAS)
    return jnp.where(values < 0.0, -power, power).astype(jnp.bfloat16)


def from_code(code, scale):
    power = code.astype(jnp.float32)
    size = (jnp.log(jnp.abs(power)) * (1.0 / math.log(2.0)) + BIAS) * (scale * (1.0 / SPAN))
    return jnp.where(power < 0.0, -size, size)


def short_rows(ext, taps_spec, fwd, inv):
    count = taps_spec.shape[0] // 2
    rows, cols = ext.shape
    starts = range(0, rows - count, count)
    wide = jnp.concatenate([ext[s : s + 2 * count] for s in starts], 1)
    spec = dot(fwd[0], wide) + dot(fwd[1], wide)
    t_re = jnp.concatenate([taps_spec[:count]] * len(starts), 1)
    t_im = jnp.concatenate([taps_spec[count:]] * len(starts), 1)
    s_re, s_im = spec[:count], spec[count:]
    prod = jnp.concatenate([s_re * t_re - s_im * t_im, s_re * t_im + s_im * t_re], 0)
    back = dot3(inv, prod)
    return jnp.concatenate([back[:, w * cols : (w + 1) * cols] for w in range(len(starts))], 0)


IN_VMEM = pl.BlockSpec(memory_space=pltpu.VMEM)
IN_SMEM = pl.BlockSpec(memory_space=pltpu.SMEM)
IN_ANY = pl.BlockSpec(memory_space=pl.ANY)
IN_HBM = pl.BlockSpec(memory_space=pltpu.HBM)


def kernel_params(mib):
    return pltpu.CompilerParams(vmem_limit_bytes=mib * MIB)


def cost(scale):
    return pl.CostEstimate(flops=0, bytes_accessed=0, transcendentals=0)


def lanes_of(slab):
    return pl.ds(pl.multiple_of(slab * LANES, LANES), LANES)


def pace_body(me, out):
    out[0] = me[0]


def pace_call(me):
    return pl.pallas_call(
        pace_body,
        in_specs=[IN_SMEM],
        out_specs=IN_SMEM,
        out_shape=jax.ShapeDtypeStruct((1,), jnp.int32),
        compiler_params=kernel_params(4),
        cost_estimate=pl.CostEstimate(flops=10_000_000_000, bytes_accessed=8, transcendentals=0),
        name="pace",
    )(me)


def main_body(me, value, gate, taps, fwd, inv, gated, spec_out):
    count = taps.shape[0]
    wide = 2 * LANES
    for c in range(0, value.shape[1], wide):
        cols = slice(c, c + wide)
        taps_spec = dot3(fwd[:, :, :count], taps[:, cols])
        spec_out[:, cols] = taps_spec
        short = short_rows(value[:, cols], taps_spec, fwd, inv)
        gated[:, cols] = gate[count:, cols].astype(jnp.float32) * short


def main_call(me, value, gate, taps, fwd, inv, after):
    rows, chans = value.shape
    count = taps.shape[0]
    return pl.pallas_call(
        drop_after(main_body, 6, len(after)),
        in_specs=[IN_SMEM] + [IN_VMEM] * 5 + [IN_ANY] * len(after),
        out_specs=[IN_VMEM] * 2,
        out_shape=[
            jax.ShapeDtypeStruct((rows - count, chans), jnp.float32),
            jax.ShapeDtypeStruct((2 * count, chans), jnp.float32),
        ],
        compiler_params=kernel_params(12),
        cost_estimate=cost(4),
        name="short_main",
    )(me, value, gate, taps, fwd, inv, *after)


def drop_after(body, keep, unused):
    return lambda *refs: body(*refs[:keep], *refs[keep + unused :])


def write_code(code, values, filter_rows):
    groups = 8
    rows = sum(v.shape[0] for v in values)
    peak = functools.reduce(
        jnp.maximum, [jnp.max(jnp.abs(v), axis=0, keepdims=True) for v in values]
    )
    scale = scale_of(peak)
    start = 0
    for v in values:
        code[start : start + v.shape[0]] = to_code(v, scale)
        start += v.shape[0]
    scale = jnp.broadcast_to(scale, (groups, LANES))
    size = jnp.abs(filter_rows)
    many = filter_rows.shape[0] // groups
    most = size[:groups]
    for c in range(1, many):
        most = jnp.maximum(most, size[c * groups : (c + 1) * groups])
    filter_scale = scale_of(jnp.max(most, axis=1, keepdims=True))
    filter_scale = jnp.broadcast_to(filter_scale, (groups, LANES))
    row, lane = (lax.broadcasted_iota(jnp.int32, scale.shape, k) for k in (0, 1))
    by_lane = jnp.sum(jnp.where(row == lane, filter_scale, 0.0), axis=0, keepdims=True)
    both = jnp.where(row == groups - 1, by_lane, scale)
    end = rows + filter_rows.shape[0]
    code[rows:end] = to_code(filter_rows, jnp.concatenate([filter_scale] * many, 0))
    rows = end
    code[rows:] = both.astype(jnp.bfloat16)


def head_body(part, me, halo, value, gate, gated, taps_spec, long_taps, fwd, inv, *outs):
    taps = halo.shape[0]
    tops, codes = outs[: len(part)], outs[len(part) :]
    for d, top, code in zip(part, tops, codes):
        slab = me[0] ^ d
        cols = lanes_of(slab)
        ext = jnp.concatenate([halo[:, cols], value[:taps, cols]], 0)
        short = short_rows(ext, taps_spec[:, cols], fwd, inv)
        first = gate[:taps, cols].astype(jnp.float32) * short
        top[...] = first
        write_code(code, [first, gated[:, cols]], long_taps[slab])


def head_call(part, me, halo, value, gate, gated, taps_spec, long_taps, fwd, inv, after):
    taps = halo.shape[0]
    whole = taps + gated.shape[0] + TILE + long_taps.shape[1]
    codes = [jax.ShapeDtypeStruct((whole, LANES), jnp.bfloat16)] * len(part)
    top = jax.ShapeDtypeStruct((taps, LANES), jnp.float32)
    return pl.pallas_call(
        drop_after(functools.partial(head_body, part), 9, len(after)),
        in_specs=[IN_SMEM] + [IN_VMEM] * 8 + [IN_ANY] * len(after),
        out_specs=[IN_VMEM] * (2 * len(part)),
        out_shape=[top] * len(part) + codes,
        compiler_params=kernel_params(12),
        cost_estimate=cost(len(part)),
        name="short_head",
    )(me, halo, value, gate, gated, taps_spec, long_taps, fwd, inv, *after)


def forward_body(d, clear, me, code, fwd, turn, widen, *rest):
    spec_out, filter_out, held_x, held_h = rest[-4:]
    rows = held_x.shape[0]
    half = rows // 2
    groups = 8
    scales = code[code.shape[0] - TILE :].astype(jnp.float32)
    held_x[...] = from_code(code[:rows], scales[:1])
    row, lane = (lax.broadcasted_iota(jnp.int32, scales.shape, k) for k in (0, 1))
    by_lane = jnp.where(row == lane, scales[groups - 1 :], 0.0)
    scale = jnp.broadcast_to(jnp.sum(by_lane, axis=1, keepdims=True), scales.shape)
    taps = code[rows : code.shape[0] - TILE]
    many = taps.shape[0] // groups
    h_high, h_low = split(from_code(taps, jnp.concatenate([scale] * many, 0)))
    h_high, h_low = h_high.astype(jnp.float32), h_low.astype(jnp.float32)
    pieces = []
    for c in range(many):
        at = slice(c * groups, (c + 1) * groups)
        pieces += [h_high[at], h_low[at]]
    wide = dot(jnp.concatenate(pieces, 0).T.astype(jnp.bfloat16), widen[...])
    for c in range(many):
        for k in range(2):
            at = (2 * c + k) * LANES
            held_h[k, c * LANES : (c + 1) * LANES] = wide[:, at : at + LANES]
    highs, lows = [], []
    for odd in range(2):
        step = pl.ds(odd, half, stride=2)
        high, low = split(held_x[step])
        highs += [high, held_h[0, step].astype(jnp.bfloat16)]
        lows += [low, held_h[1, step].astype(jnp.bfloat16)]
    width = 4 * LANES
    both = dot(fwd[0], jnp.concatenate(highs + lows, 1))
    both = both[:, :width] + both[:, width:] + dot(fwd[1], jnp.concatenate(highs, 1))
    w_re, w_im = turn[:half], turn[half:]
    outs = []
    for at in range(2):
        even = both[:, at * LANES : (at + 1) * LANES]
        odd = both[:, (2 + at) * LANES : (3 + at) * LANES]
        o_re, o_im = odd[:half], odd[half:]
        t_re = o_re * w_re - o_im * w_im
        t_im = o_re * w_im + o_im * w_re
        outs.append((even[:half] + t_re, even[:half] - t_re, even[half:] + t_im, even[half:] - t_im))
    for c, piece in enumerate(outs[0]):
        spec_out[c * half : (c + 1) * half] = piece
    if clear:
        filter_out[...] = jnp.zeros_like(filter_out)
    own = me[0] ^ d
    later = jnp.where(own + 1 < filter_out.shape[0] - 2, own + 1, own + 2)
    odd = lax.broadcasted_iota(jnp.int32, (half, LANES), 0) % 2 == 1
    for c, piece in enumerate(outs[1]):
        filter_out[own, c * half : (c + 1) * half] += piece
        moved = jnp.where(odd, -piece, piece) if c < 2 else jnp.where(odd, piece, -piece)
        at = slice(((c + 2) % 4) * half, ((c + 2) % 4 + 1) * half)
        filter_out[later, at] += moved


def forward_call(d, count, me, code, fwd, turn, widen, early, so_far, after):
    rows = 2 * fwd.shape[2]
    held = so_far + early
    return pl.pallas_call(
        functools.partial(forward_body, d, not so_far),
        in_specs=[IN_SMEM] + [IN_VMEM] * (4 + len(held)) + [IN_ANY] * len(after),
        out_specs=[IN_VMEM] * 2,
        out_shape=[
            jax.ShapeDtypeStruct((2 * rows, LANES), jnp.float32),
            jax.ShapeDtypeStruct((count + 2, 2 * rows, LANES), jnp.float32),
        ],
        scratch_shapes=[
            pltpu.VMEM((rows, LANES), jnp.float32),
            pltpu.VMEM((2, rows, LANES), jnp.float32),
        ],
        input_output_aliases={5: 1} if so_far else {},
        compiler_params=kernel_params(12),
        cost_estimate=cost(1),
        name="forward",
    )(me, code, fwd, turn, widen, *held, *after)


def back_body(part, count, me_ref, filt, inv, turn, *refs):
    specs, codes, total, held = refs[:count], refs[-2 - len(part) : -2], refs[-2], refs[-1]
    rows = held.shape[0]
    half = rows // 2
    me = me_ref[0]

    for e, code in zip(part, codes):
        lags = []
        for d in range(count):
            lag = (me ^ e) - (me ^ d)
            lags.append(jnp.where(lag >= 0, lag, count))

        def chunk(c, _):
            def piece(start):
                return pl.ds(pl.multiple_of(start + c * 8, 8), 8)

            sums = []
            for start in (0, half):
                re, im = piece(start), piece(rows + start)
                acc_re = jnp.zeros((8, LANES), jnp.float32)
                acc_im = acc_re
                for d in range(count):
                    x_re, x_im = specs[d][re], specs[d][im]
                    g_re, g_im = filt[lags[d], re], filt[lags[d], im]
                    acc_re += x_re * g_re - x_im * g_im
                    acc_im += x_re * g_im + x_im * g_re
                sums += [acc_re, acc_im]
            a_re, a_im, b_re, b_im = sums
            re, im = piece(0), piece(half)
            w_re, w_im = turn[re], turn[im]
            d_re, d_im = a_re - b_re, a_im - b_im
            total[re, :LANES] = a_re + b_re
            total[im, :LANES] = a_im + b_im
            total[re, LANES:] = d_re * w_re + d_im * w_im
            total[im, LANES:] = d_im * w_re - d_re * w_im
            return 0

        lax.fori_loop(0, half // 8, chunk, 0, unroll=8)
        values = dot3(inv, total[...])
        held[pl.ds(0, half, stride=2)] = values[:, :LANES]
        held[pl.ds(1, half, stride=2)] = values[:, LANES:]
        peak = jnp.max(jnp.abs(values), axis=0, keepdims=True)
        scale = scale_of(jnp.maximum(peak[:, :LANES], peak[:, LANES:]))
        code[:rows] = to_code(held[...], scale)
        code[rows:] = jnp.broadcast_to(scale, (TILE, LANES)).astype(jnp.bfloat16)


def back_call(part, me, filt, inv, turn, specs, after):
    count = len(specs)
    bins = specs[0].shape[0]
    code = jax.ShapeDtypeStruct((bins // 2 + TILE, LANES), jnp.bfloat16)
    return pl.pallas_call(
        functools.partial(back_body, part, count),
        in_specs=[IN_SMEM] + [IN_VMEM] * (3 + count) + [IN_ANY] * len(after),
        out_specs=[IN_VMEM] * len(part),
        out_shape=[code] * len(part),
        scratch_shapes=[
            pltpu.VMEM((bins // 2, 2 * LANES), jnp.float32),
            pltpu.VMEM((bins // 2, LANES), jnp.float32),
        ],
        compiler_params=kernel_params(12),
        cost_estimate=cost(len(part)),
        name="back",
    )(me, filt, inv, turn, *specs, *after)


def finish(code, top, gated, gate, skip, cols, out):
    taps = top.shape[0]
    rows = gate.shape[0]
    scale = code[rows : rows + 1].astype(jnp.float32)
    for r, part_gated in ((slice(0, taps), top[...]), (slice(taps, rows), gated[:, cols])):
        total = from_code(code[r], scale) + skip[:, cols] * part_gated
        out[r] = (gate[r, cols].astype(jnp.float32) * total).astype(jnp.bfloat16)


def final_body(part, me, gated, gate, skip, *refs):
    many = len(part)
    codes, tops, outs = refs[:many], refs[many : 2 * many], refs[2 * many :]
    for d, code, top, out in zip(part, codes, tops, outs):
        finish(code, top, gated, gate, skip, lanes_of(me[0] ^ d), out)


def final_call(part, me, codes, tops, gated, gate, skip, after):
    many = len(part)
    slab = jax.ShapeDtypeStruct((gate.shape[0], LANES), jnp.bfloat16)
    return pl.pallas_call(
        drop_after(functools.partial(final_body, part), 4 + 2 * many, len(after)),
        in_specs=[IN_SMEM] + [IN_VMEM] * (3 + 2 * many) + [IN_ANY] * len(after),
        out_specs=[IN_VMEM] * many,
        out_shape=[slab] * many,
        compiler_params=kernel_params(12),
        cost_estimate=cost(many),
        name="final",
    )(me, gated, gate, skip, *codes, *tops, *after)


def last_body(part, ready, me, gated, gate, skip, *refs):
    many = len(part)
    codes, tops = refs[:many], refs[many : 2 * many]
    slabs, (out, held, sems) = refs[2 * many : -3], refs[-3:]
    copies = []

    def send(d, slab):
        at = len(copies)
        copies.append(pltpu.make_async_copy(slab, out.at[:, lanes_of(me[0] ^ d)], sems.at[at]))
        copies[-1].start()

    for d, slab in zip(ready, slabs):
        send(d, slab)
    for at, d in enumerate(part):
        finish(codes[at], tops[at], gated, gate, skip, lanes_of(me[0] ^ d), held.at[at])
        send(d, held.at[at])
    for copy in copies:
        copy.wait()


def last_call(part, me, codes, tops, gated, gate, skip, slabs):
    many = len(part)
    ready = tuple(slabs)
    return pl.pallas_call(
        functools.partial(last_body, part, ready),
        in_specs=[IN_SMEM] + [IN_VMEM] * (3 + 2 * many + len(ready)),
        out_specs=IN_ANY,
        out_shape=jax.ShapeDtypeStruct(gate.shape, jnp.bfloat16),
        scratch_shapes=[
            pltpu.VMEM((many, gate.shape[0], LANES), jnp.bfloat16),
            pltpu.SemaphoreType.DMA((many + len(ready),)),
        ],
        compiler_params=kernel_params(12),
        cost_estimate=cost(many),
        name="last",
    )(me, gated, gate, skip, *codes, *tops, *slabs.values())


def in_slabs(output_gate, input_gate, value_input, short_filter, long_filter, skip_gain):
    count = lax.axis_size("ctx")
    me = lax.axis_index("ctx").reshape(1)
    rows = value_input.shape[0]
    taps = short_filter.shape[0]
    groups = long_filter.shape[1] // count

    def exchanged(block, d):
        return lax.ppermute(block, "ctx", [(i, i ^ d) for i in range(count)]) if d else block

    def table(values):
        return jnp.asarray(split_table(values))

    paced = pace_call(me)
    start = rows - taps + jnp.minimum(paced[0], 0)
    halo = passed_along(lax.dynamic_slice_in_dim(value_input, start, taps, 0), "ctx", 1)
    long_taps = long_filter.T.reshape(count, groups, rows // LANES, LANES)
    long_taps = jnp.swapaxes(long_taps, 1, 2).reshape(count, -1, LANES)

    forward, inverse = tables(taps)
    short_fwd, short_inv = table(forward), table(inverse[taps:])
    half = rows // 2
    forward, inverse = tables(half)
    fwd, inv = table(forward[:, :half]), table(inverse[:half] / 2)
    turn = jnp.asarray(turning(rows, LANES))
    widen = jnp.asarray(widening(groups, LANES, 2 * rows // LANES))

    came, tops, specs, answers = {}, {}, {}, {}
    after, filt, mixed = [], [], {}

    main_out = []

    def mains():
        main_out[:] = main_call(
            paced, value_input, input_gate, short_filter, short_fwd, short_inv, after
        )
        after[:] = main_out[:1]

    def heads(*part):
        outs = head_call(
            part, me, halo, value_input, input_gate, *main_out, long_taps,
            short_fwd, short_inv, after,
        )
        after[:] = outs[:1]
        for d, top, code in zip(part, outs, outs[len(part) :]):
            tops[d] = top
            came[d] = exchanged(code, d)

    def forwards(*part):
        for d in part:
            specs[d], filt[:] = (lambda a, b: (a, [b]))(
                *forward_call(
                    d, count, me, came[d], fwd, turn, widen, [] if d else [inv], filt, after
                )
            )
            after[:] = [specs[d]]

    def backs(*part):
        held = [specs[d] for d in range(count)]
        for e in part:
            (code,) = back_call([e], me, filt[0], inv, turn, held, after)
            answers[e] = exchanged(code, e)
            after[:] = [code]

    def finals(*part):
        args = [me, [answers[e] for e in part], [tops[e] for e in part]]
        args += [main_out[0], output_gate, skip_gain[None]]
        if len(mixed) + len(part) == count:
            return last_call(part, *args, mixed)
        outs = final_call(part, *args, after)
        mixed.update(zip(part, outs))
        after[:] = outs[:1]

    mains()
    heads(4)
    heads(2)
    heads(5)
    heads(3)
    heads(6, 0)
    forwards(0)
    forwards(4)
    heads(1)
    forwards(2)
    heads(7)
    forwards(5)
    forwards(3)
    forwards(6)
    forwards(1)
    forwards(7)
    backs(4)
    backs(5)
    backs(6)
    backs(7)
    backs(3)
    backs(0)
    finals(0, 4)
    backs(2)
    finals(5)
    backs(1)
    finals(6, 7)
    return finals(3, 2, 1)


def local(output_gate, input_gate, value_input, short_filter, long_filter, skip_gain):
    count = lax.axis_size("ctx")
    rows, chans = value_input.shape
    taps = short_filter.shape[0]
    groups = long_filter.shape[1]
    fits = chans == LANES * count and groups == 8 * count and taps == LANES
    fits = fits and rows % (2 * LANES) == 0 and rows > taps and count & (count - 1) == 0
    run = in_slabs if fits else plain
    return run(output_gate, input_gate, value_input, short_filter, long_filter, skip_gain)


def solution(mesh):
    placed = (
        P("ctx", "ch"),
        P("ctx", "ch"),
        P("ctx", "ch"),
        P(None, "ch"),
        P("ctx", "ch"),
        P("ch"),
    )
    return jax.shard_map(
        local, mesh=mesh, in_specs=placed, out_specs=P("ctx", "ch"), check_vma=False
    )
```
